128 devices in a mesh: fsdp: 32 (over y, z_lo, x), tp: 4 (over z_hi, core).
Axes of the slice: x: 4, y: 4, z: 4 (z_hi: 2, z_lo: 2; z = z_hi * 2 + z_lo), core: 2. Of those that a mesh axis runs over, the one named last changes fastest.
Arguments:
- ref_rows: bfloat16 [1024, 4096], P(('fsdp', 'tp')), may hold values from -6 to 6
- ref_gain: float32 [4096], replicated, may hold values from 0.5 to 1.5
- trainee_rows: bfloat16 [1024, 8192], P('fsdp', 'tp'), may hold values from -6 to 6
- trainee_gain: float32 [8192], replicated, may hold values from 0.5 to 1.5
- ref_head: bfloat16 [4096, 65536], P(None, ('fsdp', 'tp'))
- trainee_head: bfloat16 [8192, 65536], P(None, ('fsdp', 'tp'))
- targets: int32 [1024], replicated, may hold values from 0 to 65535
- selected: int32 [1024], replicated, may hold values 0 or 1
Outputs:
- excess: float32 [1024], P(('fsdp', 'tp'))
- head_grad: bfloat16 [8192, 65536], P(None, ('fsdp', 'tp'))
The draws below stay inside these ranges and needn't reach their ends.
All inputs are finite; a program needn't handle non-finite values.
Results may differ from the reference program's by a relative error of at most 0.0051.
Values may be sent and summed in bfloat16 or wider, within the bound.
No kernel may reach another device: no remote copies, remote signals or barrier semaphores. Data moves between devices by JAX's collectives and lax.ppermute only.
A program may use at most 128 MiB of HBM per device.

```python
import math
import jax
import jax.numpy as jnp
import numpy as np
from jax import lax

D = 8192
DR = 4096
V = 65536
TOKENS = 1024


def draw_ref_rows(key, part):
    key = jax.random.fold_in(key, 1)
    values = jnp.clip(jax.random.normal(key, (TOKENS, DR), jnp.float32), -6.0, 6.0)
    return values.astype(jnp.bfloat16)


def draw_trainee_rows(key, part):
    key = jax.random.fold_in(key, 2)
    values = jnp.clip(jax.random.normal(key, (TOKENS, D), jnp.float32), -6.0, 6.0)
    return values.astype(jnp.bfloat16)


def draw_ref_head(key, part):
    key = jax.random.fold_in(key, 3)
    values = jnp.clip(jax.random.normal(key, (DR, V), jnp.float32), -6.0, 6.0) * (3.0 / math.sqrt(DR))
    return values.astype(jnp.bfloat16)


def draw_trainee_head(key, part):
    key = jax.random.fold_in(key, 4)
    values = jnp.clip(jax.random.normal(key, (D, V), jnp.float32), -6.0, 6.0) * (3.0 / math.sqrt(D))
    return values.astype(jnp.bfloat16)


def place_ends(drawn, stream_key, least, largest):
    longest = drawn.shape.index(max(drawn.shape))
    spots = []
    for shift in (0, 1):
        where = [jax.random.randint(jax.random.fold_in(stream_key, axis), (), 0, length) for axis, length in enumerate(drawn.shape)]
        where[longest] = (where[longest] + shift) % drawn.shape[longest]
        spots.append(tuple(where))
    return drawn.at[spots[0]].set(least).at[spots[1]].set(largest)


def cumulative_ranks(amount, slope):
    weights = [(1 << 20) // math.isqrt(standing ** slope) + 1 for standing in range(1, amount + 1)]
    deviation = 1 + sum(weights) // (1 << 30)
    return np.cumsum(np.array([max(1, weight // deviation) for weight in weights]))


def ranked(key, dims, count, slope):
    table = cumulative_ranks(count, slope)
    ticket = jax.random.randint(jax.random.fold_in(key, 1), dims, 0, int(table[count - 1]))
    rank = jnp.searchsorted(jnp.asarray(table, jnp.int32), ticket, side="right")
    return jax.random.permutation(jax.random.fold_in(key, 2), count)[rank].astype(jnp.int32)


def setup_inputs(seed: int = 0) -> dict:
    seeds = jax.random.split(jax.random.key(seed), 9)
    return {
        "ref_rows": draw_ref_rows(jax.random.fold_in(seeds[8], 71), 0),
        "ref_gain": jnp.clip(1.0 + 0.1 * jax.random.normal(seeds[1], (DR,), jnp.float32), 0.5, 1.5),
        "trainee_rows": draw_trainee_rows(jax.random.fold_in(seeds[8], 71), 0),
        "trainee_gain": jnp.clip(1.0 + 0.1 * jax.random.normal(seeds[3], (D,), jnp.float32), 0.5, 1.5),
        "ref_head": draw_ref_head(jax.random.fold_in(seeds[8], 71), 0),
        "trainee_head": draw_trainee_head(jax.random.fold_in(seeds[8], 71), 0),
        "targets": place_ends(ranked(seeds[6], (TOKENS,), V, 2), jax.random.fold_in(seeds[6], 3), 0, V - 1).astype(jnp.int32),
        "selected": place_ends((jax.random.randint(seeds[7], (TOKENS,), 0, 5) < 3).astype(jnp.int32), jax.random.fold_in(seeds[7], 1), 0, 1),
    }


EPSILON = 1e-05

def normalize(values, gain):
    widened = values.astype(jnp.float32)
    factor = lax.rsqrt(lax.optimization_barrier(jnp.mean(widened * widened, axis=1, keepdims=True)) + EPSILON)
    return (widened * factor * gain).astype(jnp.bfloat16)

def token_losses(normed, head, targets):
    logits = jnp.dot(normed, head, preferred_element_type=jnp.float32)
    highest = lax.optimization_barrier(jnp.max(logits, axis=1))
    log_total = highest + jnp.log(lax.optimization_barrier(jnp.sum(jnp.exp(logits - highest[:, None]), axis=1)))
    target_hit = jnp.take_along_axis(logits, targets[:, None], axis=1)[:, 0]
    return (log_total, target_hit)

def reference(ref_rows, ref_gain, trainee_rows, trainee_gain, ref_head, trainee_head, targets, selected):
    ref_normed = normalize(ref_rows, ref_gain)
    own_normed = normalize(trainee_rows, trainee_gain)
    ref_lse, ref_hit = token_losses(ref_normed, ref_head, targets)
    own_lse, own_hit = token_losses(own_normed, trainee_head, targets)
    excess = own_lse - own_hit - (ref_lse - ref_hit)
    weight = selected.astype(jnp.float32)
    block_count = 8
    block_width = V // block_count

    def one_block(block_index):
        start = block_index * block_width
        portion = lax.dynamic_slice_in_dim(trainee_head, start, block_width, 1)
        logits = jnp.dot(own_normed, portion, preferred_element_type=jnp.float32)
        column = start + jnp.arange(block_width, dtype=jnp.int32)
        onehot = (targets[:, None] == column[None, :]).astype(jnp.float32)
        scaled = (weight[:, None] * (jnp.exp(logits - own_lse[:, None]) - onehot)).astype(jnp.bfloat16)
        return lax.dot_general(own_normed, scaled, (((0,), (0,)), ((), ())), preferred_element_type=jnp.float32).astype(jnp.bfloat16)
    blocks = lax.map(one_block, jnp.arange(block_count, dtype=jnp.int32))
    head_grad = jnp.transpose(blocks, (1, 0, 2)).reshape(D, V)
    return (excess, head_grad)
```

```python
import jax
import jax.numpy as jnp
from jax import lax
from jax.sharding import PartitionSpec as P

EPSILON = 1e-05
ALL = ("fsdp", "tp")
OFFSETS = ((0, -1, 1, 2), (0, 1, -1, 2))
OWN_PARTS = ((0, 3, "yzx"), (3, 6, "zxy"), (6, 8, "xyz"))
REF_PARTS = ((0, 3, "xyz"), (3, 6, "yzx"), (6, 8, "zxy"))


def flat(x, y, z, core):
    return (((y % 4) * 2 + (z % 4) % 2) * 4 + (x % 4)) * 4 + ((z % 4) // 2) * 2 + core


def place(index):
    x = (index // 4) % 4
    y = index // 32
    z = ((index // 2) % 2) * 2 + (index // 16) % 2
    return x, y, z, index % 2


def shifted(axis, steps):
    pairs = []
    for index in range(128):
        x, y, z, core = place(index)
        at = {"x": x, "y": y, "z": z}
        at[axis] += steps[core]
        pairs.append((index, flat(at["x"], at["y"], at["z"], core)))
    return pairs


def send(values, axis, steps):
    return lax.ppermute(values, ALL, shifted(axis, steps))


def swap(values):
    return lax.ppermute(values, ALL, [(index, index ^ 1) for index in range(128)])


def normalize(values, gain):
    widened = values.astype(jnp.float32)
    factor = lax.rsqrt(jnp.mean(widened * widened, axis=1, keepdims=True) + EPSILON)
    return (widened * factor * gain).astype(jnp.bfloat16)


def spread(rows, axis, forward):
    first = send(rows, axis, (1, -1))
    second = send(rows, axis, (-1, 1))
    third = send(first, axis, (1, -1)) if forward else send(rows, axis, (2, 2))
    return rows, first, second, third


def gather(rows, parts):
    early, late = [], []
    level = [rows[low:high] for low, high, _ in parts]
    for stage in (0, 1):
        level = [
            jnp.concatenate(spread(piece, order[stage], False), axis=0)
            for piece, (_, _, order) in zip(level, parts)
        ]
    for piece, (_, _, order) in zip(level, parts):
        *most, last = spread(piece, order[2], True)
        early += most
        late.append(last)
    early += [swap(piece) for piece in early]
    late += [swap(piece) for piece in late]
    return jnp.concatenate(early, axis=0), jnp.concatenate(late, axis=0)


def token_ids(parts):
    me = lax.axis_index(ALL)
    x, y, z, my_core = place(me)
    here = {"x": x, "y": y, "z": z}
    offsets = jnp.asarray(OFFSETS, jnp.int32)
    early, late = [], []
    for core in (my_core, 1 - my_core):
        off = jnp.where(core == 0, offsets[0], offsets[1])
        for low, high, order in parts:
            shape = (4, 4, 4, high - low)
            at = {}
            for dim, axis in enumerate((order[2], order[1], order[0])):
                along = off.reshape([4 if d == dim else 1 for d in range(4)])
                at[axis] = here[axis] + along + 4
            row = jnp.arange(low, high, dtype=jnp.int32).reshape(1, 1, 1, -1)
            ids = jnp.broadcast_to(8 * flat(at["x"], at["y"], at["z"], core) + row, shape)
            ids = ids.reshape(4, -1)
            early.append(ids[:3].reshape(-1))
            late.append(ids[3])
    return jnp.concatenate(early), jnp.concatenate(late)


def pick(values, ids):
    hit = ids[:, None] == jnp.arange(1024, dtype=jnp.int32)[None, :]
    return jnp.sum(jnp.where(hit, values[None, :], jnp.zeros((), values.dtype)), axis=1)


def unpick(values, ids):
    hit = ids[None, :] == jnp.arange(1024, dtype=jnp.int32)[:, None]
    return jnp.sum(jnp.where(hit, values[None, :], jnp.zeros((), values.dtype)), axis=1)


def local_stats(logits, wanted, first_column):
    column = first_column + jnp.arange(logits.shape[1], dtype=jnp.int32)
    highest = jnp.max(logits, axis=1)
    summed = jnp.sum(jnp.exp(logits - highest[:, None]), axis=1)
    hit = jnp.sum(jnp.where(wanted[:, None] == column[None, :], logits, 0.0), axis=1)
    return highest + jnp.log(summed), hit


def join(terms):
    peak = terms[0]
    for term in terms[1:]:
        peak = jnp.maximum(peak, term)
    return peak + jnp.log(sum(jnp.exp(term - peak) for term in terms))


def everywhere(values, combine):
    values = combine([values, swap(values)])
    for axis in "xyz":
        values = combine([values] + [send(values, axis, (s, s)) for s in (1, -1, 2)])
    return values


def shards(
    ref_rows, ref_gain, trainee_rows, trainee_gain, ref_head, trainee_head, targets, selected
):
    me = lax.axis_index(ALL)
    first_column = me * trainee_head.shape[1]

    rows = lax.all_to_all(trainee_rows.reshape(4, 8, 2048), "tp", 0, 0)
    rows = jnp.concatenate([rows[i] for i in range(4)], axis=1)
    own_early, own_late = gather(normalize(rows, trainee_gain), OWN_PARTS)
    ref_early, ref_late = gather(normalize(ref_rows, ref_gain), REF_PARTS)

    own_ids = token_ids(OWN_PARTS)
    ref_ids = token_ids(REF_PARTS)
    own_all = jnp.concatenate(own_ids)
    ref_all = jnp.concatenate(ref_ids)
    wanted = pick(targets, own_all)
    ref_wanted = pick(targets, ref_all)
    chosen = pick(selected, own_all)

    n = own_early.shape[0]

    def logits_of(early, late, head):
        return [jnp.dot(part, head, preferred_element_type=jnp.float32) for part in (early, late)]

    own_logits = logits_of(own_early, own_late, trainee_head)
    own_stats = [
        local_stats(part, want, first_column)
        for part, want in zip(own_logits, (wanted[:n], wanted[n:]))
    ]
    own_lse = unpick(jnp.concatenate([s[0] for s in own_stats]), own_all)
    own_hit = unpick(jnp.concatenate([s[1] for s in own_stats]), own_all)
    own_lse = everywhere(own_lse.reshape(8, 128), join).reshape(1024)

    ref_logits = logits_of(ref_early, ref_late, ref_head)
    ref_stats = [
        local_stats(part, want, first_column)
        for part, want in zip(ref_logits, (ref_wanted[:n], ref_wanted[n:]))
    ]
    ref_lse = unpick(jnp.concatenate([s[0] for s in ref_stats]), ref_all)
    ref_hit = unpick(jnp.concatenate([s[1] for s in ref_stats]), ref_all)

    def combine(terms):
        return jnp.stack([join([t[0] for t in terms]), sum(t[1] for t in terms)])

    total = everywhere(
        jnp.stack([ref_lse.reshape(8, 128), (own_hit - ref_hit).reshape(8, 128)]), combine
    ).reshape(2, 1024)
    excess = own_lse - total[0] - total[1]

    lse = pick(own_lse, own_all)
    weight = chosen.astype(jnp.float32)
    column = first_column + jnp.arange(trainee_head.shape[1], dtype=jnp.int32)
    onehot = (wanted[:, None] == column[None, :]).astype(jnp.float32)
    logits = jnp.concatenate(own_logits, axis=0)
    scaled = (weight[:, None] * (jnp.exp(logits - lse[:, None]) - onehot)).astype(jnp.bfloat16)
    own_normed = jnp.concatenate([own_early, own_late], axis=0)
    head_grad = lax.dot_general(
        own_normed, scaled, (((0,), (0,)), ((), ())), preferred_element_type=jnp.float32
    ).astype(jnp.bfloat16)
    return lax.dynamic_slice_in_dim(excess, me * 8, 8), head_grad


def solution(mesh):
    in_specs = (P(ALL, None), P(), P("fsdp", "tp"), P(), P(None, ALL), P(None, ALL), P(), P())
    out_specs = (P(ALL), P(None, ALL))
    return jax.shard_map(shards, mesh=mesh, in_specs=in_specs, out_specs=out_specs, check_vma=False)
```

```python
import functools

import jax
import jax.numpy as jnp
from jax import lax
from jax.experimental import pallas as pl
from jax.experimental.pallas import tpu as pltpu
from jax.sharding import PartitionSpec as P

EPSILON = 1e-05
ALL = ("fsdp", "tp")
ORDERS = ("yzx", "zxy", "xyz")
WIDE = 4096
TOKENS = 1024
MIB = 1 << 20
BLOCK = 1024
DEEP = 512


def flat(x, y, z, core):
    return (((y % 4) * 2 + (z % 4) % 2) * 4 + (x % 4)) * 4 + ((z % 4) // 2) * 2 + core


def place(index):
    x = (index // 4) % 4
    y = index // 32
    z = ((index // 2) % 2) * 2 + (index // 16) % 2
    return x, y, z, index % 2


def shifted(axis, steps):
    pairs = []
    for index in range(128):
        x, y, z, core = place(index)
        at = {"x": x, "y": y, "z": z}
        at[axis] += steps[core]
        pairs.append((index, flat(at["x"], at["y"], at["z"], core)))
    return pairs


def send(values, axis, steps):
    return lax.ppermute(values, ALL, shifted(axis, steps))


def exchange(values, bits):
    return lax.ppermute(values, ALL, [(index, index ^ bits) for index in range(128)])


def normalize(values, gain):
    widened = values.astype(jnp.float32)
    factor = lax.rsqrt(jnp.mean(widened * widened, axis=1, keepdims=True) + EPSILON)
    return (widened * factor * gain).astype(jnp.bfloat16)


def gather(parts):
    level = parts
    for stage in (0, 1):
        grown = []
        for rows, order in zip(level, ORDERS):
            axis = order[stage]
            near = [send(rows, axis, steps) for steps in ((1, -1), (-1, 1), (2, 2))]
            grown.append(jnp.concatenate([rows, *near], axis=0))
        level = grown
    slots = []
    firsts = [send(rows, order[2], (1, -1)) for rows, order in zip(level, ORDERS)]
    seconds = [send(rows, order[2], (-1, 1)) for rows, order in zip(level, ORDERS)]
    thirds = [send(rows, order[2], (1, -1)) for rows, order in zip(firsts, ORDERS)]
    for mine in zip(level, firsts, seconds, thirds):
        slots.append([*mine, *(exchange(piece, 1) for piece in mine)])
    return slots


def row_table(me):
    here = place(me)
    t = jnp.arange(3 * 8 * 16, dtype=jnp.int32)
    part, slot, group = t // 128, (t // 16) % 8, t % 16
    core = jnp.where(slot >= 4, 1 - here[3], here[3])

    def offset(j):
        return jnp.where(j == 0, 0, jnp.where(j == 3, 2, (2 * j - 3) * (1 - 2 * core)))

    along = (offset(group % 4), offset(group // 4), offset(slot % 4))
    at = []
    for axis, start in zip("xyz", here):
        step = jnp.zeros_like(t)
        for number, order in enumerate(ORDERS):
            step = jnp.where(part == number, along[order.index(axis)], step)
        at.append(start + step + 4)
    return 8 * flat(*at, core)


def copy_in(pieces, head, at, xbuf, hbuf, sems):
    copies = []
    for number, piece in enumerate(pieces):
        copies.append(
            pltpu.make_async_copy(
                piece, xbuf.at[at, pl.ds(128 * number, 128), :], sems.at[at, number]
            )
        )
    copies.append(pltpu.make_async_copy(head, hbuf.at[at], sems.at[at, len(pieces)]))
    for copy in copies:
        copy.start()
    return copies


def add_logits(at, slots, table, xbuf, hbuf, tmp, total):
    rows = 128 * len(slots)
    tmp[pl.ds(0, rows), :] = jnp.zeros((rows, 512), jnp.float32)

    def deep(step, carry):
        cut = pl.ds(pl.multiple_of(step * DEEP, DEEP), DEEP)
        tmp[pl.ds(0, rows), :] += jnp.dot(
            xbuf[at, pl.ds(0, rows), cut], hbuf[at, cut, :], preferred_element_type=jnp.float32
        )
        return carry

    lax.fori_loop(0, WIDE // DEEP, deep, 0)
    for number, slot in enumerate(slots):

        def place_rows(group, carry):
            first = pl.multiple_of(table[(at * 8 + slot) * 16 + group], 8)
            source = pl.multiple_of(128 * number + 8 * group, 8)
            total[min(at, 2) // 2, pl.ds(first, 8), :] += tmp[pl.ds(source, 8), :]
            return carry

        lax.fori_loop(0, 16, place_rows, 0, unroll=4)


EARLY = (0, 4, 1, 5, 2, 6)
LATE = (3, 7)


def early_kernel(table, *refs):
    pieces, (own_head, ref_head, total, xbuf, hbuf, tmp, sems) = refs[:18], refs[18:]
    heads = (own_head.at[pl.ds(0, WIDE), :], own_head.at[pl.ds(WIDE, WIDE), :], ref_head)
    waits = [copy_in(pieces[6 * k : 6 * k + 6], heads[k], k, xbuf, hbuf, sems) for k in range(3)]
    total[...] = jnp.zeros_like(total)
    for k in range(3):
        for copy in waits[k]:
            copy.wait()
        add_logits(k, EARLY, table, xbuf, hbuf, tmp, total)


def late_kernel(table, *refs):
    pieces = refs[:6]
    own_head, ref_head, before, info, total, stats, xbuf, hbuf, tmp, sems = refs[6:]
    heads = (own_head.at[pl.ds(0, WIDE), :], own_head.at[pl.ds(WIDE, WIDE), :], ref_head)
    copy = pltpu.make_async_copy(before, total, sems.at[3, 0])
    copy.start()
    waits = [copy_in(pieces[2 * k : 2 * k + 2], heads[k], k, xbuf, hbuf, sems) for k in range(3)]
    copy.wait()
    for k in range(3):
        for copy in waits[k]:
            copy.wait()
        add_logits(k, LATE, table, xbuf, hbuf, tmp, total)

    def chunk(step, carry):
        rows = pl.ds(pl.multiple_of(step * 128, 128), 128)
        wanted = jnp.transpose(info[:, rows])[:, 0:1]
        column = lax.broadcasted_iota(jnp.int32, (128, 512), 1).astype(jnp.float32)
        found = []
        for which in (0, 1):
            logits = total[which, rows, :]
            peak = jnp.max(logits, axis=1, keepdims=True)
            summed = jnp.sum(jnp.exp(logits - peak), axis=1, keepdims=True)
            hit = jnp.sum(jnp.where(column == wanted, logits, 0.0), axis=1, keepdims=True)
            found.append((peak + jnp.log(summed), hit))
        lane = lax.broadcasted_iota(jnp.int32, (128, 128), 1)
        block = jnp.where(
            lane == 0,
            found[0][0],
            jnp.where(lane == 1, found[1][0], jnp.where(lane == 2, found[0][1] - found[1][1], 0.0)),
        )
        stats[:, rows] = jnp.transpose(block)[0:8, :]
        return carry

    lax.fori_loop(0, TOKENS // 128, chunk, 0)


def grad_kernel(table, *refs):
    pieces, (logits, joined, info, out, plain, ordered, scaled) = refs[:16], refs[16:]
    step = pl.program_id(0)
    half = WIDE // BLOCK

    @pl.when(step == 0)
    def _():
        def chunk(number, carry):
            rows = pl.ds(pl.multiple_of(number * 128, 128), 128)
            told = jnp.transpose(info[:, rows])
            lse = jnp.transpose(joined[:, rows])[:, 0:1]
            column = lax.broadcasted_iota(jnp.int32, (128, 512), 1).astype(jnp.float32)
            hit = (column == told[:, 0:1]).astype(jnp.float32)
            plain[rows, :] = told[:, 1:2] * (jnp.exp(logits[0, rows, :] - lse) - hit)
            return carry

        lax.fori_loop(0, TOKENS // 128, chunk, 0)
        for part in (0, 1):

            def place_rows(group, carry):
                first = pl.multiple_of(table[part * 128 + group], 8)
                ordered[pl.ds(pl.multiple_of(8 * group, 8), 8), :] = plain[pl.ds(first, 8), :]
                return carry

            lax.fori_loop(0, 128, place_rows, 0, unroll=8)
            scaled[part] = ordered[...].astype(jnp.bfloat16)

    for part in (0, 1):

        @pl.when(step // half == part)
        def _():
            rows = jnp.concatenate([piece[...] for piece in pieces[8 * part : 8 * part + 8]], axis=0)
            out[...] = lax.dot_general(
                rows, scaled[part], (((0,), (0,)), ((), ())), preferred_element_type=jnp.float32
            ).astype(jnp.bfloat16)


ANY = pl.BlockSpec(memory_space=pl.ANY)
INSIDE = pl.BlockSpec(memory_space=pltpu.VMEM)
TABLE = pl.BlockSpec(memory_space=pltpu.SMEM)


def logits_call(kernel, slots, table, pieces, heads, extra, out_shape, extra_specs):
    rows = 128 * len(slots)
    outs = jax.tree.map(lambda _: INSIDE, out_shape)
    return pl.pallas_call(
        kernel,
        out_shape=out_shape,
        in_specs=[TABLE] + [ANY] * (len(pieces) + 2) + extra_specs,
        out_specs=outs,
        scratch_shapes=[
            pltpu.VMEM((3, rows, WIDE), jnp.bfloat16),
            pltpu.VMEM((3, WIDE, 512), jnp.bfloat16),
            pltpu.VMEM((rows, 512), jnp.float32),
            pltpu.SemaphoreType.DMA((4, len(slots) + 1)),
        ],
        compiler_params=pltpu.CompilerParams(vmem_limit_bytes=48 * MIB),
        cost_estimate=pl.CostEstimate(
            flops=2 * 3 * rows * WIDE * 512,
            bytes_accessed=3 * (rows * WIDE * 2 + WIDE * 1024) + 4 * MIB,
            transcendentals=0,
        ),
    )(table, *pieces, *heads, *extra)


def grad_call(table, pieces, logits, joined, info):
    half = WIDE // BLOCK
    first = pl.BlockSpec((128, BLOCK), lambda b: (0, jnp.minimum(b, half - 1)))
    second = pl.BlockSpec((128, BLOCK), lambda b: (0, jnp.maximum(b - half, 0)))
    return pl.pallas_call(
        grad_kernel,
        grid=(2 * half,),
        out_shape=jax.ShapeDtypeStruct((2 * WIDE, 512), jnp.bfloat16),
        in_specs=[TABLE]
        + [first] * 8
        + [second] * 8
        + [pl.BlockSpec((1, TOKENS, 512), lambda b: (0, 0, 0))]
        + [pl.BlockSpec((8, TOKENS), lambda b: (0, 0))] * 2,
        out_specs=pl.BlockSpec((BLOCK, 512), lambda b: (b, 0)),
        scratch_shapes=[
            pltpu.VMEM((TOKENS, 512), jnp.float32),
            pltpu.VMEM((TOKENS, 512), jnp.float32),
            pltpu.VMEM((2, TOKENS, 512), jnp.bfloat16),
        ],
        compiler_params=pltpu.CompilerParams(vmem_limit_bytes=48 * MIB),
        cost_estimate=pl.CostEstimate(
            flops=2 * TOKENS * 2 * WIDE * 512, bytes_accessed=26 * MIB, transcendentals=0
        ),
    )(table, *pieces, logits, joined, info)


def join(terms):
    peak = functools.reduce(jnp.maximum, terms)
    logs = peak + jnp.log(sum(jnp.exp(term - peak) for term in terms))
    row = lax.broadcasted_iota(jnp.int32, peak.shape, 0)
    return jnp.where(row < 2, logs, sum(terms))


def everywhere(values):
    values = join([values, exchange(values, 1)])
    for axis in "xyz":
        values = join([values] + [send(values, axis, (s, s)) for s in (1, -1, 2)])
    return values


def own_rows(block, member):
    arrived = []
    for bits in range(4):
        there = member ^ bits
        cut = lax.dynamic_slice_in_dim(block, 8 * there, 8)
        arrived.append(exchange(cut, bits) if bits else cut)
    quarters = []
    for quarter in range(4):
        found = arrived[0]
        for bits in (1, 2, 3):
            found = jnp.where((member ^ bits) == quarter, arrived[bits], found)
        quarters.append(found)
    return jnp.concatenate(quarters, axis=1)


def shards(
    ref_rows, ref_gain, trainee_rows, trainee_gain, ref_head, trainee_head, targets, selected
):
    me = lax.axis_index(ALL)
    own = normalize(own_rows(trainee_rows, lax.axis_index("tp")), trainee_gain)
    ref = normalize(ref_rows, ref_gain)
    slots = gather([own[:, :WIDE], own[:, WIDE:], ref])

    table = row_table(me)
    wanted = (targets - me * trainee_head.shape[1]).astype(jnp.float32)
    row = lax.broadcasted_iota(jnp.int32, (8, TOKENS), 0)
    info = jnp.where(
        row == 0, wanted[None], jnp.where(row == 1, selected.astype(jnp.float32)[None], 0.0)
    )

    totals = jax.ShapeDtypeStruct((2, TOKENS, 512), jnp.float32)
    heads = (trainee_head, ref_head)
    early = [part[slot] for part in slots for slot in EARLY]
    late = [part[slot] for part in slots for slot in LATE]
    before = logits_call(early_kernel, EARLY, table, early, heads, (), totals, [])
    logits, stats = logits_call(
        late_kernel,
        LATE,
        table,
        late,
        heads,
        (before, info),
        (totals, jax.ShapeDtypeStruct((8, TOKENS), jnp.float32)),
        [ANY, INSIDE],
    )
    joined = everywhere(stats)
    excess = joined[0] - joined[1] - joined[2]
    head_grad = grad_call(table, [*slots[0], *slots[1]], logits, joined, info)
    return lax.dynamic_slice_in_dim(excess, me * 8, 8), head_grad


def solution(mesh):
    in_specs = (P(ALL, None), P(), P("fsdp", "tp"), P(), P(None, ALL), P(None, ALL), P(), P())
    out_specs = (P(ALL), P(None, ALL))
    return jax.shard_map(shards, mesh=mesh, in_specs=in_specs, out_specs=out_specs, check_vma=False)
```

```python
import jax
import jax.numpy as jnp
from jax import lax
from jax.experimental import pallas as pl
from jax.experimental.pallas import tpu as pltpu
from jax.sharding import Mesh
from jax.sharding import PartitionSpec as P

EPSILON = 1e-05
FSDP = ("y", "zl", "x")
TP = ("zh", "c")
ALL = (*FSDP, *TP)
CHIPS = ALL[:-1]
WIDE = 4096
HALF = 512
BLOCK = 1024
MIB = 1 << 20
NEAR, BACK = (1, -1), (-1, 1)


def flat(x, y, z, core):
    return (((y % 4) * 2 + (z % 4) % 2) * 4 + (x % 4)) * 4 + ((z % 4) // 2) * 2 + core


def place(index):
    x = (index // 4) % 4
    y = index // 32
    z = ((index // 2) % 2) * 2 + (index // 16) % 2
    return x, y, z, index % 2


def send(values, axis, steps):
    pairs = []
    for index in range(128):
        x, y, z, core = place(index)
        at = {"x": x, "y": y, "z": z}
        at[axis] += steps[core]
        pairs.append((index, flat(at["x"], at["y"], at["z"], core)))
    return lax.ppermute(values, ALL, pairs)


def swap(values):
    return lax.ppermute(values, ALL, [(index, index ^ 1) for index in range(128)])


def ring(rows, axis):
    return jnp.concatenate(
        [rows, *(send(rows, axis, steps) for steps in (NEAR, BACK, (2, 2)))], axis=0
    )


def fence(*values):
    return lax.optimization_barrier(values)


def normalize(values, gain):
    widened = values.astype(jnp.float32)
    factor = lax.rsqrt(jnp.mean(widened * widened, axis=1, keepdims=True) + EPSILON)
    return (widened * factor * gain).astype(jnp.bfloat16)


def row_table(me):
    x, y, z, mine = place(me)
    t = jnp.arange(3 * 8 * 16, dtype=jnp.int32)
    part, slot, group = t // 128, (t // 16) % 8, t % 16
    core = jnp.where(slot >= 4, 1 - mine, mine)

    def offset(j):
        return jnp.where(j == 0, 0, jnp.where(j == 3, 2, (2 * j - 3) * (1 - 2 * core))) + 4

    last, outer, inner = offset(slot % 4), offset(group // 4), offset(group % 4)
    at_x = (x + jnp.where(part == 0, last, outer)) % 4
    at_y = (y + jnp.where(part == 0, outer, jnp.where(part == 1, last, inner))) % 4
    at_z = (z + last) % 4
    low = jnp.where(part == 2, at_z % 2, group // 2 % 2)
    high = jnp.where(part == 2, at_z // 2, group % 2)
    return 8 * (((at_y * 2 + low) * 4 + at_x) * 2 + high)


def start_copies(sources, targets, sems):
    copies = [
        pltpu.make_async_copy(source, target, sems.at[number])
        for number, (source, target) in enumerate(zip(sources, targets))
    ]
    for copy in copies:
        copy.start()
    return copies


def put_rows(table, first, tmp, rows, total, lanes, add):
    for group in range(rows // 8):
        target = pl.ds(pl.multiple_of(table[first + group], 8), 8)
        values = tmp[8 * group : 8 * group + 8, :]
        if add:
            total[target, lanes] += values
        else:
            total[target, lanes] = values


def stats_of(total, info):
    def chunk(step):
        rows = pl.ds(pl.multiple_of(step * 128, 128), 128)
        told = jnp.transpose(info[:, rows])
        column = lax.broadcasted_iota(jnp.int32, (128, HALF), 1).astype(jnp.float32)
        sides = [total[rows, pl.ds(HALF * side, HALF)] for side in (0, 1)]
        peaks = [jnp.max(side, axis=1, keepdims=True) for side in sides]
        peak = jnp.maximum(*peaks)
        summed = sum(jnp.sum(jnp.exp(side - peak), axis=1, keepdims=True) for side in sides)
        hit = sum(
            jnp.sum(
                jnp.where(column == told[:, number : number + 1], side, 0.0), axis=1, keepdims=True
            )
            for number, side in enumerate(sides)
        )
        lane = lax.broadcasted_iota(jnp.int32, (128, 128), 1)
        block = jnp.where(lane == 0, peak + jnp.log(summed), jnp.where(lane == 1, hit, 0.0))
        return rows, jnp.transpose(block)[0:8, :]

    return chunk


def ref_kernel(table, *refs):
    pieces, (head, head_2, info, stats, xbuf, hbuf, tmp, total, sems) = refs[:4], refs[4:]
    copies = start_copies(
        [*pieces, head, head_2],
        [*(xbuf.at[pl.ds(128 * k, 128), :] for k in range(4)), hbuf.at[0], hbuf.at[1]],
        sems,
    )
    for copy in copies[:5]:
        copy.wait()
    for side in (0, 1):
        if side:
            copies[5].wait()
        for pair in (0, 1):
            tmp[...] = jnp.dot(
                xbuf[256 * pair : 256 * pair + 256, :],
                hbuf[side],
                preferred_element_type=jnp.float32,
            )
            lanes = pl.ds(HALF * side, HALF)
            put_rows(table, 256 + 32 * pair, tmp, 256, total, lanes, False)
    chunk = stats_of(total, info)

    def body(step, carry):
        rows, block = chunk(step)
        stats[:, rows] = block
        return carry

    lax.fori_loop(0, HALF // 128, body, 0)


def early_kernel(table, *refs):
    pieces, (head, head_2, total, xbuf, hbuf, tmp, sems) = refs[:6], refs[6:]
    copies = []
    for part in (0, 1):
        cut = pl.ds(WIDE * part, WIDE)
        sources = [*pieces[3 * part : 3 * part + 3], head.at[cut, :], head_2.at[cut, :]]
        targets = [xbuf.at[part, pl.ds(128 * k, 128), :] for k in range(3)]
        targets += [hbuf.at[part, 0], hbuf.at[part, 1]]
        copies.append(start_copies(sources, targets, sems.at[part]))
    total[...] = jnp.zeros_like(total)
    for part in (0, 1):
        for copy in copies[part][:4]:
            copy.wait()
        for side in (0, 1):
            if side:
                copies[part][4].wait()
            tmp[...] = jnp.dot(
                xbuf[part], hbuf[part, side], preferred_element_type=jnp.float32
            )
            put_rows(table, 128 * part, tmp, 384, total, pl.ds(HALF * side, HALF), True)


def late_kernel(table, *refs):
    pieces = refs[:2]
    head, head_2, before, info, mine, other, stats, xbuf, hbuf, tmp, total, sems = refs[2:]
    copies = []
    for part in (0, 1):
        cut = pl.ds(WIDE * part, WIDE)
        sources = [pieces[part], head.at[cut, :], head_2.at[cut, :]]
        targets = [xbuf.at[part], hbuf.at[part, 0], hbuf.at[part, 1]]
        copies.append(start_copies(sources, targets, sems.at[part]))
    copy = pltpu.make_async_copy(before, total, sems.at[2, 0])
    copy.start()
    for part in (0, 1):
        for number in (0, 1):
            copies[part][number].wait()
        for side in (0, 1):
            if side:
                copies[part][2].wait()
            tmp[...] = jnp.dot(
                xbuf[part], hbuf[part, side], preferred_element_type=jnp.float32
            )
            if part == 0 and side == 0:
                copy.wait()
            put_rows(table, 128 * part + 48, tmp, 128, total, pl.ds(HALF * side, HALF), True)
    chunk = stats_of(total, info)

    def body(step, carry):
        rows, block = chunk(step)
        stats[:, rows] = block
        mine[rows, :] = total[rows, pl.ds(0, HALF)]
        other[rows, :] = total[rows, pl.ds(HALF, HALF)]
        return carry

    lax.fori_loop(0, HALF // 128, body, 0)


def grad_kernel(table, *refs):
    pieces = refs[:16]
    mine, other, info, lses, out, xbuf, obuf, plain, ordered, scaled, sems, out_sems = refs[16:]
    copies = [
        start_copies(
            pieces[8 * part : 8 * part + 8],
            [xbuf.at[part, pl.ds(128 * k, 128), :] for k in range(8)],
            sems.at[part],
        )
        for part in (0, 1)
    ]

    for core, logits in enumerate((mine, other)):

        def chunk(number, carry):
            source = pl.ds(pl.multiple_of(number * 128, 128), 128)
            rows = pl.ds(pl.multiple_of(number * 128 + HALF * core, 128), 128)
            told = jnp.transpose(info[:, rows])
            lse = lses[pl.ds(number + 4 * core, 1), :]
            lse = jnp.transpose(jnp.broadcast_to(lse, (8, 128)))[:, 0:1]
            column = lax.broadcasted_iota(jnp.int32, (128, HALF), 1).astype(jnp.float32)
            hit = (column == told[:, 0:1]).astype(jnp.float32)
            plain[rows, :] = told[:, 2:3] * (jnp.exp(logits[source, :] - lse) - hit)
            return carry

        lax.fori_loop(0, HALF // 128, chunk, 0)
    for part in (0, 1):
        for core in (0, 1):

            def place_rows(group, carry):
                source = table[part * 128 + core * 64 + group] + HALF * core
                target = pl.multiple_of(HALF * core + 8 * group, 8)
                ordered[pl.ds(target, 8), :] = plain[pl.ds(pl.multiple_of(source, 8), 8), :]
                return carry

            lax.fori_loop(0, 64, place_rows, 0, unroll=16)
        scaled[part] = ordered[...].astype(jnp.bfloat16)
    steps = WIDE // BLOCK
    sent = []
    for part in (0, 1):
        for copy in copies[part]:
            copy.wait()
        for step in range(steps):
            number = part * steps + step
            if number >= 2:
                sent[number - 2].wait()
            obuf[number % 2] = lax.dot_general(
                xbuf[part, :, BLOCK * step : BLOCK * step + BLOCK],
                scaled[part],
                (((0,), (0,)), ((), ())),
                preferred_element_type=jnp.float32,
            ).astype(jnp.bfloat16)
            sent.append(
                pltpu.make_async_copy(
                    obuf.at[number % 2],
                    out.at[pl.ds(BLOCK * number, BLOCK), :],
                    out_sems.at[number % 2],
                )
            )
            sent[number].start()
    for copy in sent[-2:]:
        copy.wait()


ANY = pl.BlockSpec(memory_space=pl.ANY)
INSIDE = pl.BlockSpec(memory_space=pltpu.VMEM)
TABLE = pl.BlockSpec(memory_space=pltpu.SMEM)
DMA = pltpu.SemaphoreType.DMA


def floats(*shape):
    return jax.ShapeDtypeStruct(shape, jnp.float32)


def call(kernel, operands, specs, out_shape, out_specs, scratch, limit, flops, moved):
    return pl.pallas_call(
        kernel,
        out_shape=out_shape,
        in_specs=[TABLE, *specs],
        out_specs=out_specs,
        scratch_shapes=scratch,
        compiler_params=pltpu.CompilerParams(vmem_limit_bytes=limit * MIB),
        cost_estimate=pl.CostEstimate(
            flops=flops, bytes_accessed=moved * MIB, transcendentals=0
        ),
    )(*operands)


def ref_call(table, pieces, heads, info):
    scratch = [
        pltpu.VMEM((HALF, WIDE), jnp.bfloat16),
        pltpu.VMEM((2, WIDE, HALF), jnp.bfloat16),
        pltpu.VMEM((256, HALF), jnp.float32),
        pltpu.VMEM((HALF, 2 * HALF), jnp.float32),
        DMA((6,)),
    ]
    flops = 4 * HALF * HALF * WIDE
    specs = [ANY] * 6 + [INSIDE]
    operands = (table, *pieces, *heads, info)
    return call(ref_kernel, operands, specs, floats(8, HALF), INSIDE, scratch, 20, flops, 12)


def early_call(table, pieces, heads):
    scratch = [
        pltpu.VMEM((2, 384, WIDE), jnp.bfloat16),
        pltpu.VMEM((2, 2, WIDE, HALF), jnp.bfloat16),
        pltpu.VMEM((384, HALF), jnp.float32),
        DMA((2, 5)),
    ]
    flops = 8 * 384 * HALF * WIDE
    specs = [ANY] * 8
    operands = (table, *pieces, *heads)
    shape = floats(HALF, 2 * HALF)
    return call(early_kernel, operands, specs, shape, INSIDE, scratch, 28, flops, 24)


def late_call(table, pieces, heads, before, info):
    scratch = [
        pltpu.VMEM((2, 128, WIDE), jnp.bfloat16),
        pltpu.VMEM((2, 2, WIDE, HALF), jnp.bfloat16),
        pltpu.VMEM((128, HALF), jnp.float32),
        pltpu.VMEM((HALF, 2 * HALF), jnp.float32),
        DMA((3, 3)),
    ]
    flops = 8 * 128 * HALF * WIDE
    specs = [ANY] * 5 + [INSIDE]
    operands = (table, *pieces, *heads, before, info)
    shapes = (floats(HALF, HALF), floats(HALF, HALF), floats(8, HALF))
    return call(late_kernel, operands, specs, shapes, (INSIDE,) * 3, scratch, 26, flops, 20)


def grad_call(table, pieces, logits, info, lses):
    scratch = [
        pltpu.VMEM((2, 2 * HALF, WIDE), jnp.bfloat16),
        pltpu.VMEM((2, BLOCK, HALF), jnp.bfloat16),
        pltpu.VMEM((2 * HALF, HALF), jnp.float32),
        pltpu.VMEM((2 * HALF, HALF), jnp.float32),
        pltpu.VMEM((2, 2 * HALF, HALF), jnp.bfloat16),
        DMA((2, 8)),
        DMA((2,)),
    ]
    flops = 2 * 2 * HALF * 2 * WIDE * HALF
    specs = [ANY] * 16 + [INSIDE] * 4
    operands = (table, *pieces, *logits, info, lses)
    shape = jax.ShapeDtypeStruct((2 * WIDE, HALF), jnp.bfloat16)
    return call(grad_kernel, operands, specs, shape, ANY, scratch, 32, flops, 26)


def log_sum(terms, axis):
    peak = jnp.max(terms, axis=axis)
    return peak + jnp.log(jnp.sum(jnp.exp(terms - jnp.expand_dims(peak, axis)), axis=axis))


def core_tokens(values, core):
    values = values.reshape(64, 2, 8)
    return jnp.where(core == 0, values[:, 0], values[:, 1]).reshape(HALF)


def shards(
    ref_rows, ref_gain, trainee_rows, trainee_gain, ref_head, trainee_head, targets, selected
):
    me = lax.axis_index(ALL)
    core = lax.axis_index("c")
    chip = me // 2

    raw = trainee_rows.reshape(2, 2, 8, 2048).transpose(1, 0, 2, 3).reshape(1, 1, 2, 16, 2048)
    raw = jnp.broadcast_to(raw, (2, 2, 2, 16, 2048)).reshape(8, 16, 2048)
    raw = lax.all_to_all(raw, ("zl", "zh", "c"), 0, 0, tiled=True).reshape(2, 4, 16, 2048)
    own = normalize(raw.transpose(0, 2, 1, 3).reshape(32, 2 * WIDE), trainee_gain)
    ref = ring(ring(normalize(ref_rows, ref_gain), "y"), "x")
    ref_near, ref_back = send(ref, "z", NEAR), send(ref, "z", BACK)
    head_2, ref_head_2 = swap(trainee_head), swap(ref_head)
    own, head_2, ref_head_2 = fence(own, head_2, ref_head_2)

    low, top = ring(own[:, :WIDE], "y"), ring(own[:, WIDE:], "x")
    low, top = fence(low, top)

    low_near, top_near = send(low, "x", NEAR), send(top, "y", NEAR)
    low_back = send(low, "x", BACK)
    top, ref_near, ref_back = fence(top, ref_near, ref_back)
    top_back = send(top, "y", BACK)
    ref_far = send(ref_near, "z", NEAR)

    table = row_table(me)
    weight = selected.astype(jnp.float32)

    def info_of(which):
        wanted = core_tokens(targets, which)
        row = lax.broadcasted_iota(jnp.int32, (8, HALF), 0)
        beside = (wanted - HALF * (me ^ 1)).astype(jnp.float32)
        here = (wanted - HALF * me).astype(jnp.float32)
        rest = jnp.where(row == 1, beside[None], core_tokens(weight, which)[None])
        return jnp.where(row == 0, here[None], rest)

    info, info_2 = info_of(core), info_of(1 - core)
    ref_pieces = (ref, ref_near, ref_back, ref_far)
    ref_stats = ref_call(table, ref_pieces, (ref_head, ref_head_2), info)

    low, low_near, low_back, top, top_near, top_back, ref_stats = fence(
        low, low_near, low_back, top, top_near, top_back, ref_stats
    )
    low_far, top_far = send(low_near, "x", NEAR), send(top_near, "y", NEAR)
    early = (low, low_near, low_back, top, top_near, top_back)
    before = early_call(table, early, (trainee_head, head_2))
    low_2, top_2, low_near_2 = swap(low), swap(top), swap(low_near)
    low_far, top_far, before, low_2, top_2, low_near_2 = fence(
        low_far, top_far, before, low_2, top_2, low_near_2
    )
    mine, other, stats = late_call(
        table, (low_far, top_far), (trainee_head, head_2), before, info
    )

    rest = jnp.concatenate(
        [ref_stats[0].reshape(64, 8), (stats[1] - ref_stats[1]).reshape(64, 8)], axis=1
    )
    rest = jnp.pad(rest, ((0, 0), (0, 112)))
    message = jnp.concatenate(
        [jnp.broadcast_to(stats[0].reshape(1, 4, 128), (64, 4, 128)), rest[:, None]], axis=1
    )
    message, other, top_near, low_back, top_back, low_far, top_far = fence(
        message, other, top_near, low_back, top_back, low_far, top_far
    )
    arrived = lax.all_to_all(message, CHIPS, 0, 0, tiled=True)
    other_2 = swap(other)
    top_near_2, low_back_2, top_back_2 = swap(top_near), swap(low_back), swap(top_back)
    low_far_2, top_far_2 = swap(low_far), swap(top_far)
    lse = log_sum(arrived[:, :4], 0)
    lse_2 = swap(lse)
    found = log_sum(arrived[:, 4, :8], 0)
    hits = jnp.sum(arrived[:, 4, 8:16], axis=0)
    excess = lax.dynamic_slice_in_dim(lse.reshape(HALF), 8 * chip, 8) - found - hits

    pieces = (low, low_near, low_back, low_far, low_2, low_near_2, low_back_2, low_far_2)
    pieces += (top, top_near, top_back, top_far, top_2, top_near_2, top_back_2, top_far_2)
    head_grad = grad_call(
        table,
        pieces,
        (mine, other_2),
        jnp.concatenate([info, info_2], axis=1),
        jnp.concatenate([lse, lse_2], axis=0),
    )
    return excess, head_grad


def solution(mesh):
    grid = Mesh(mesh.devices.reshape(4, 2, 4, 2, 2), ALL)
    in_specs = (P(ALL, None), P(), P(FSDP, TP), P(), P(None, ALL), P(None, ALL), P(), P())
    out_specs = (P(ALL), P(None, ALL))
    return jax.shard_map(shards, mesh=grid, in_specs=in_specs, out_specs=out_specs, check_vma=False)
```

```python
import jax
import jax.numpy as jnp
from jax import lax
from jax.experimental import pallas as pl
from jax.experimental.pallas import tpu as pltpu
from jax.sharding import Mesh
from jax.sharding import PartitionSpec as P

EPSILON = 1e-05
FSDP = ("y", "zl", "x")
TP = ("zh", "c")
ALL = (*FSDP, *TP)
CHIPS = ALL[:-1]
WIDE = 4096
HALF = 512
BLOCK = 1024
MIB = 1 << 20


def flat(x, y, z, core):
    return (((y % 4) * 2 + (z % 4) % 2) * 4 + (x % 4)) * 4 + ((z % 4) // 2) * 2 + core


def place(index):
    x = (index // 4) % 4
    y = index // 32
    z = ((index // 2) % 2) * 2 + (index // 16) % 2
    return x, y, z, index % 2


def send(values, axes, steps):
    pairs = []
    for index in range(128):
        x, y, z, core = place(index)
        at = {"x": x, "y": y, "z": z}
        at[axes[core]] += steps[core]
        pairs.append((index, flat(at["x"], at["y"], at["z"], core)))
    return lax.ppermute(values, ALL, pairs)


def swap(values):
    return lax.ppermute(values, ALL, [(index, index ^ 1) for index in range(128)])


def ring(rows, axes):
    return [rows, *(send(rows, axes, (steps, steps)) for steps in (1, -1, 2))]


def stack(pieces, cut=slice(None)):
    return jnp.concatenate([piece[:, cut] for piece in pieces], axis=0)


def fence(*values):
    return lax.optimization_barrier(values)


def normalize(values, gain):
    widened = values.astype(jnp.float32)
    factor = lax.rsqrt(jnp.mean(widened * widened, axis=1, keepdims=True) + EPSILON)
    return (widened * factor * gain).astype(jnp.bfloat16)


def row_table(me):
    x, y, z, mine = place(me)
    t = jnp.arange(2 * 8 * 16, dtype=jnp.int32)
    part, slot, group = t // 128, (t // 16) % 8, t % 16
    core = jnp.where(slot >= 4, 1 - mine, mine)

    def offset(j):
        return jnp.where(j == 0, 0, jnp.where(j == 3, 2, 2 * j - 3)) + 4

    last, outer, inner = offset(slot % 4), offset(group // 4), offset(group % 4)
    first, second = jnp.where(part == 0, outer, inner), jnp.where(part == 0, last, outer)
    at_x = (x + jnp.where(core == 0, first, second)) % 4
    at_y = (y + jnp.where(core == 0, second, first)) % 4
    at_z = (z + jnp.where(core == 0, last, 8 - last)) % 4
    low = jnp.where(part == 1, at_z % 2, group // 2 % 2)
    high = jnp.where(part == 1, at_z // 2, group % 2)
    return 8 * (((at_y * 2 + low) * 4 + at_x) * 2 + high)


def put_rows(table, first, values, total):
    for group in range(16):
        target = pl.ds(pl.multiple_of(table[first + group], 8), 8)
        total[target, :] = values[8 * group : 8 * group + 8, :]


def write_stats(sides, info, stats):
    column = lax.broadcasted_iota(jnp.int32, (128, HALF), 1).astype(jnp.float32)
    lane = lax.broadcasted_iota(jnp.int32, (128, 128), 1)
    for step in range(HALF // 128):
        rows = slice(128 * step, 128 * step + 128)
        told = jnp.transpose(info[:, rows])
        values = [side[rows, :] for side in sides]
        peaks = [jnp.max(value, axis=1, keepdims=True) for value in values]
        peak = jnp.maximum(*peaks)
        summed = jnp.sum(sum(jnp.exp(value - peak) for value in values), axis=1, keepdims=True)
        hits = [
            jnp.where(column == told[:, number : number + 1], value, 0.0)
            for number, value in enumerate(values)
        ]
        hit = jnp.sum(sum(hits), axis=1, keepdims=True)
        block = jnp.where(lane == 0, peak + jnp.log(summed), jnp.where(lane == 1, hit, 0.0))
        stats[:, rows] = jnp.transpose(block)[0:8, :]


def start(copies):
    for copy in copies:
        copy.start()


def wait(copies):
    for copy in copies:
        copy.wait()


def copies_of(sources, targets, sems):
    return [
        pltpu.make_async_copy(source, target, sems.at[k])
        for k, (source, target) in enumerate(zip(sources, targets))
    ]


def put_slots(table, first, tmp, total):
    for slot in range(tmp.shape[0] // 128):
        put_rows(table, first + 16 * slot, tmp[128 * slot : 128 * slot + 128, :], total)


def early_kernel(table, *refs):
    pieces, (head, head_2, mine, other, xbuf, tmp, sems) = refs[:6], refs[6:]
    places = [pl.ds(128 * k, 128) for k in range(3)]
    arrive = [
        copies_of(pieces[part::2], [xbuf.at[part, place, :] for place in places], sems.at[part])
        for part in (0, 1)
    ]
    start(arrive[0])
    start(arrive[1])
    wait(arrive[0])
    for side, columns in enumerate((head, head_2)):
        tmp[side] = jnp.dot(xbuf[0], columns[0:WIDE, :], preferred_element_type=jnp.float32)
    wait(arrive[1])
    for side, (columns, total) in enumerate(((head, mine), (head_2, other))):
        tmp[side] += jnp.dot(
            xbuf[1], columns[WIDE : 2 * WIDE, :], preferred_element_type=jnp.float32
        )
        put_slots(table, 0, tmp.at[side], total)


def ref_kernel(table, *refs):
    pieces, (head, head_2, mine, other, xbuf, hbuf, tmp, sems) = refs[:3], refs[3:]
    targets = [xbuf.at[pl.ds(128 * k, 128), :] for k in range(3)]
    arrive = copies_of((*pieces, head, head_2), (*targets, hbuf.at[0], hbuf.at[1]), sems)
    start(arrive)
    wait(arrive[:4])
    for side, total in enumerate((mine, other)):
        if side:
            wait(arrive[4:])
        tmp[...] = jnp.dot(xbuf[...], hbuf[side], preferred_element_type=jnp.float32)
        put_slots(table, 128, tmp, total)


def ref_late_kernel(table, *refs):
    far, head, head_2, mine, other, info, stats, xbuf, hbuf, totals, tmp, sems = refs
    sources = (far, head, mine, other, head_2)
    arrive = copies_of(sources, (xbuf, hbuf.at[0], totals.at[0], totals.at[1], hbuf.at[1]), sems)
    start(arrive)
    wait(arrive[:4])
    for side in (0, 1):
        if side:
            wait(arrive[4:])
        tmp[...] = jnp.dot(xbuf[...], hbuf[side], preferred_element_type=jnp.float32)
        put_slots(table, 176, tmp, totals.at[side])
    write_stats((totals.at[0], totals.at[1]), info, stats)


def late_kernel(table, *refs):
    low, top, head, head_2, mine_0, other_0, info, mine, other, stats, xbuf, tmp, sems = refs
    arrive = copies_of((low, top), (xbuf.at[0], xbuf.at[1]), sems)
    start(arrive)
    mine[...], other[...] = mine_0[...], other_0[...]
    wait(arrive)
    for columns, total in ((head, mine), (head_2, other)):
        tmp[...] = jnp.dot(xbuf[0], columns[0:WIDE, :], preferred_element_type=jnp.float32)
        tmp[...] += jnp.dot(
            xbuf[1], columns[WIDE : 2 * WIDE, :], preferred_element_type=jnp.float32
        )
        put_slots(table, 48, tmp, total)
    write_stats((mine, other), info, stats)


def grad_kernel(table, *refs):
    pieces, (mine, other, lse, lse_2, info, out) = refs[:16], refs[16:22]
    xbuf, obuf, plain, ordered, scaled, sems, out_sems = refs[22:]
    logits = [
        pltpu.make_async_copy(source, plain.at[pl.ds(HALF * k, HALF), :], sems.at[2, k])
        for k, source in enumerate((mine, other))
    ]
    start(logits)
    arrive = []
    for part in (0, 1):
        sources = pieces[part::2]
        arrive.append(
            [
                pltpu.make_async_copy(
                    source, xbuf.at[part, pl.ds(128 * k, 128), :], sems.at[part, k]
                )
                for k, source in enumerate(sources)
            ]
        )
    start(arrive[0])
    wait(logits)
    column = lax.broadcasted_iota(jnp.int32, (128, HALF), 1).astype(jnp.float32)
    for step in range(2 * HALF // 128):
        rows = slice(128 * step, 128 * step + 128)
        told = jnp.transpose(info[:, rows])
        joined = lse[step : step + 1, :] if step < 4 else lse_2[step - 4 : step - 3, :]
        joined = jnp.transpose(jnp.broadcast_to(joined, (8, 128)))[:, 0:1]
        hit = (column == told[:, 0:1]).astype(jnp.float32)
        plain[rows, :] = told[:, 2:3] * (jnp.exp(plain[rows, :] - joined) - hit)
    for group in range(128):
        source = pl.multiple_of(table[group] + HALF * (group // 64), 8)
        ordered[8 * group : 8 * group + 8, :] = plain[pl.ds(source, 8), :]
    scaled[...] = ordered[...].astype(jnp.bfloat16)
    steps = WIDE // BLOCK
    sent = []
    for part in (0, 1):
        wait(arrive[part])
        if part == 0:
            start(arrive[1])
        for step in range(steps):
            number = part * steps + step
            if number >= 2:
                sent[number - 2].wait()
            obuf[number % 2] = lax.dot_general(
                xbuf[part, :, BLOCK * step : BLOCK * step + BLOCK],
                scaled[...],
                (((0,), (0,)), ((), ())),
                preferred_element_type=jnp.float32,
            ).astype(jnp.bfloat16)
            sent.append(
                pltpu.make_async_copy(
                    obuf.at[number % 2],
                    out.at[pl.ds(BLOCK * number, BLOCK), :],
                    out_sems.at[number % 2],
                )
            )
            sent[number].start()
    wait(sent[-2:])


ANY = pl.BlockSpec(memory_space=pl.ANY)
INSIDE = pl.BlockSpec(memory_space=pltpu.VMEM)
TABLE = pl.BlockSpec(memory_space=pltpu.SMEM)
DMA = pltpu.SemaphoreType.DMA


def floats(*shape):
    return jax.ShapeDtypeStruct(shape, jnp.float32)


def call(kernel, operands, out_shape, out_specs, scratch, rows, specs, limit=40):
    return pl.pallas_call(
        kernel,
        out_shape=out_shape,
        in_specs=[TABLE, *specs],
        out_specs=out_specs,
        scratch_shapes=scratch,
        compiler_params=pltpu.CompilerParams(vmem_limit_bytes=limit * MIB),
        cost_estimate=pl.CostEstimate(
            flops=4 * rows * HALF * WIDE, bytes_accessed=12 * MIB, transcendentals=0
        ),
    )(*operands)


TOTALS = (floats(HALF, HALF), floats(HALF, HALF))
PRODUCT = pltpu.VMEM((128, HALF), jnp.float32)


def early_call(table, pieces, heads):
    operands = (table, *pieces, *heads)
    specs = [ANY] * 6 + [INSIDE] * 2
    scratch = [
        pltpu.VMEM((2, 384, WIDE), jnp.bfloat16),
        pltpu.VMEM((2, 384, HALF), jnp.float32),
        DMA((2, 3)),
    ]
    return call(early_kernel, operands, TOTALS, (INSIDE,) * 2, scratch, 768, specs)


def ref_call(table, pieces, heads):
    operands = (table, *pieces, *heads)
    scratch = [
        pltpu.VMEM((384, WIDE), jnp.bfloat16),
        pltpu.VMEM((2, WIDE, HALF), jnp.bfloat16),
        pltpu.VMEM((384, HALF), jnp.float32),
        DMA((5,)),
    ]
    return call(ref_kernel, operands, TOTALS, (INSIDE,) * 2, scratch, 384, [ANY] * 5)


def ref_late_call(table, far, heads, totals, info):
    operands = (table, far, *heads, *totals, info)
    scratch = [
        pltpu.VMEM((128, WIDE), jnp.bfloat16),
        pltpu.VMEM((2, WIDE, HALF), jnp.bfloat16),
        pltpu.VMEM((2, HALF, HALF), jnp.float32),
        PRODUCT,
        DMA((5,)),
    ]
    specs = [ANY] * 5 + [INSIDE]
    return call(ref_late_kernel, operands, floats(8, HALF), INSIDE, scratch, 128, specs)


def late_call(table, fars, heads, totals, info):
    operands = (table, *fars, *heads, *totals, info)
    shapes = (*TOTALS, floats(8, HALF))
    scratch = [pltpu.VMEM((2, 128, WIDE), jnp.bfloat16), PRODUCT, DMA((2,))]
    specs = [ANY] * 2 + [INSIDE] * 5
    return call(late_kernel, operands, shapes, (INSIDE,) * 3, scratch, 256, specs)


def grad_call(table, pieces, logits, lses, info):
    scratch = [
        pltpu.VMEM((2, 2 * HALF, WIDE), jnp.bfloat16),
        pltpu.VMEM((2, BLOCK, HALF), jnp.bfloat16),
        pltpu.VMEM((2 * HALF, HALF), jnp.float32),
        pltpu.VMEM((2 * HALF, HALF), jnp.float32),
        pltpu.VMEM((2 * HALF, HALF), jnp.bfloat16),
        DMA((3, 8)),
        DMA((2,)),
    ]
    operands = (table, *pieces, *logits, *lses, info)
    specs = [ANY] * 18 + [INSIDE] * 3
    shape = jax.ShapeDtypeStruct((2 * WIDE, HALF), jnp.bfloat16)
    return call(grad_kernel, operands, shape, ANY, scratch, 1024, specs, 60)


def log_sum(terms, axis):
    peak = jnp.max(terms, axis=axis)
    return peak + jnp.log(jnp.sum(jnp.exp(terms - jnp.expand_dims(peak, axis)), axis=axis))


def core_tokens(values, core):
    values = values.reshape(64, 2, 8)
    return jnp.where(core == 0, values[:, 0], values[:, 1]).reshape(HALF)


def shards(
    ref_rows, ref_gain, trainee_rows, trainee_gain, ref_head, trainee_head, targets, selected
):
    me = lax.axis_index(ALL)
    core = lax.axis_index("c")
    chip = me // 2

    table = row_table(me)
    weight = selected.astype(jnp.float32)

    def info_of(which):
        wanted = core_tokens(targets, which)
        row = lax.broadcasted_iota(jnp.int32, (8, HALF), 0)
        beside = (wanted - HALF * (me ^ 1)).astype(jnp.float32)
        here = (wanted - HALF * me).astype(jnp.float32)
        rest = jnp.where(row == 1, beside[None], core_tokens(weight, which)[None])
        return jnp.where(row == 0, here[None], rest)

    info, info_2 = info_of(core), info_of(1 - core)

    raw = trainee_rows.reshape(2, 2, 8, 2048).transpose(1, 0, 2, 3).reshape(1, 1, 2, 16, 2048)
    raw = jnp.broadcast_to(raw, (2, 2, 2, 16, 2048)).reshape(8, 16, 2048)
    raw, ref = fence(raw, normalize(ref_rows, ref_gain))
    raw = lax.all_to_all(raw, ("zl", "zh", "c"), 0, 0, tiled=True).reshape(2, 4, 16, 2048)
    own = normalize(raw.transpose(0, 2, 1, 3).reshape(32, 2 * WIDE), trainee_gain)
    ref = stack(ring(stack(ring(ref, "xy")), "yx"))
    head_2, ref_head_2 = swap(trainee_head), swap(ref_head)
    own, ref, head_2, ref_head_2 = fence(own, ref, head_2, ref_head_2)
    heads, ref_heads = (trainee_head, head_2), (ref_head, ref_head_2)

    ref_near, ref_back = send(ref, "zz", (1, -1)), send(ref, "zz", (-1, 1))
    own = ring(own, "xy")
    low, top = fence(stack(own, slice(0, WIDE)), stack(own, slice(WIDE, None)))

    low_near, low_back = send(low, "yx", (1, 1)), send(low, "yx", (-1, -1))
    top_near, top_back = send(top, "yx", (1, 1)), send(top, "yx", (-1, -1))
    ref_near, ref_back = fence(ref_near, ref_back)
    ref_far = send(ref_near, "zz", (1, -1))
    ref_totals = ref_call(table, (ref, ref_near, ref_back), ref_heads)
    low, top, low_near, top_near, low_back, top_back, ref_far, *ref_totals = fence(
        low, top, low_near, top_near, low_back, top_back, ref_far, *ref_totals
    )

    low_far, top_far = send(low_near, "yx", (1, 1)), send(top_back, "yx", (-1, -1))
    pieces = (low, top, low_near, top_near, low_back, top_back)
    totals = early_call(table, pieces, heads)
    ref_stats = ref_late_call(table, ref_far, ref_heads, ref_totals, info)
    near_2 = swap(low_near), swap(top_near)
    low_back_2 = swap(low_back)
    low_far, top_far, low_back_2, ref_stats, top_back, low, top, *rest = fence(
        low_far, top_far, low_back_2, ref_stats, top_back, low, top, *totals, *near_2
    )
    totals, near_2 = rest[:2], rest[2:]
    swapped = [swap(piece) for piece in (low, top, top_back, low_far, top_far)]
    mine, other, stats = late_call(table, (low_far, top_far), heads, totals, info)

    rest = jnp.concatenate(
        [ref_stats[0].reshape(64, 8), (stats[1] - ref_stats[1]).reshape(64, 8)], axis=1
    )
    rest = jnp.pad(rest, ((0, 0), (0, 112)))
    message = jnp.concatenate(
        [jnp.broadcast_to(stats[0].reshape(1, 4, 128), (64, 4, 128)), rest[:, None]], axis=1
    )
    message, other, *swapped = fence(message, other, *swapped)
    low_2, top_2, top_back_2, low_far_2, top_far_2 = swapped
    arrived = lax.all_to_all(message, CHIPS, 0, 0, tiled=True)
    other_2 = swap(other)
    lse = log_sum(arrived[:, :4], 0)
    lse_2 = swap(lse)
    found = log_sum(arrived[:, 4, :8], 0)
    hits = jnp.sum(arrived[:, 4, 8:16], axis=0)
    excess = lax.dynamic_slice_in_dim(lse.reshape(HALF), 8 * chip, 8) - found - hits

    pieces = (low, top, low_near, top_near, low_back, top_back, low_far, top_far)
    pieces += (low_2, top_2, *near_2, low_back_2, top_back_2, low_far_2, top_far_2)
    both = jnp.concatenate([info, info_2], axis=1)
    head_grad = grad_call(table, pieces, (mine, other_2), (lse, lse_2), both)
    return excess, head_grad


def solution(mesh):
    grid = Mesh(mesh.devices.reshape(4, 2, 4, 2, 2), ALL)
    in_specs = (P(ALL, None), P(), P(FSDP, TP), P(), P(None, ALL), P(None, ALL), P(), P())
    out_specs = (P(ALL), P(None, ALL))
    return jax.shard_map(shards, mesh=grid, in_specs=in_specs, out_specs=out_specs, check_vma=False)
```

```python
import jax
import jax.numpy as jnp
from jax import lax
from jax.experimental import pallas as pl
from jax.experimental.pallas import tpu as pltpu
from jax.sharding import Mesh
from jax.sharding import PartitionSpec as P

EPSILON = 1e-05
FSDP = ("y", "zl", "x")
TP = ("zh", "c")
ALL = (*FSDP, *TP)
CHIPS = ALL[:-1]
WIDE = 4096
HALF = 512
BLOCK = 1024
DEEP = 2048
MIB = 1 << 20


def flat(x, y, z, core):
    return (((y % 4) * 2 + (z % 4) % 2) * 4 + (x % 4)) * 4 + ((z % 4) // 2) * 2 + core


def place(index):
    x = (index // 4) % 4
    y = index // 32
    z = ((index // 2) % 2) * 2 + (index // 16) % 2
    return x, y, z, index % 2


def send(values, axes, steps):
    pairs = []
    for index in range(128):
        x, y, z, core = place(index)
        at = {"x": x, "y": y, "z": z}
        at[axes[core]] += steps[core]
        pairs.append((index, flat(at["x"], at["y"], at["z"], core)))
    return lax.ppermute(values, ALL, pairs)


def swap(values):
    return lax.ppermute(values, ALL, [(index, index ^ 1) for index in range(128)])


def ring(rows, axes):
    return [rows, *(send(rows, axes, (steps, steps)) for steps in (1, -1, 2))]


def stack(pieces, cut=slice(None)):
    return jnp.concatenate([piece[:, cut] for piece in pieces], axis=0)


def fence(*values):
    return lax.optimization_barrier(values)


def normalize(values, gain):
    widened = values.astype(jnp.float32)
    factor = lax.rsqrt(jnp.mean(widened * widened, axis=1, keepdims=True) + EPSILON)
    return (widened * factor * gain).astype(jnp.bfloat16)


def row_table(me):
    x, y, z, mine = place(me)
    t = jnp.arange(2 * 8 * 16, dtype=jnp.int32)
    part, slot, group = t // 128, (t // 16) % 8, t % 16
    core = jnp.where(slot >= 4, 1 - mine, mine)

    def offset(j):
        return jnp.where(j == 0, 0, jnp.where(j == 3, 2, 2 * j - 3)) + 4

    last, outer, inner = offset(slot % 4), offset(group // 4), offset(group % 4)
    first, second = jnp.where(part == 0, outer, inner), jnp.where(part == 0, last, outer)
    at_x = (x + jnp.where(core == 0, first, second)) % 4
    at_y = (y + jnp.where(core == 0, second, first)) % 4
    at_z = (z + jnp.where(core == 0, last, 8 - last)) % 4
    low = jnp.where(part == 1, at_z % 2, group // 2 % 2)
    high = jnp.where(part == 1, at_z // 2, group % 2)
    return 8 * (((at_y * 2 + low) * 4 + at_x) * 2 + high)


def put_rows(table, first, values, total):
    for group in range(16):
        target = pl.ds(pl.multiple_of(table[first + group], 8), 8)
        total[target, :] = values[8 * group : 8 * group + 8, :]


def write_stats(sides, info, stats):
    column = lax.broadcasted_iota(jnp.int32, (128, HALF), 1).astype(jnp.float32)
    lane = lax.broadcasted_iota(jnp.int32, (128, 128), 1)
    for step in range(HALF // 128):
        rows = slice(128 * step, 128 * step + 128)
        told = jnp.transpose(info[:, rows])
        values = [side[rows, :] for side in sides]
        peaks = [jnp.max(value, axis=1, keepdims=True) for value in values]
        peak = jnp.maximum(*peaks)
        summed = jnp.sum(sum(jnp.exp(value - peak) for value in values), axis=1, keepdims=True)
        hits = [
            jnp.where(column == told[:, number : number + 1], value, 0.0)
            for number, value in enumerate(values)
        ]
        hit = jnp.sum(sum(hits), axis=1, keepdims=True)
        block = jnp.where(lane == 0, peak + jnp.log(summed), jnp.where(lane == 1, hit, 0.0))
        stats[:, rows] = jnp.transpose(block)[0:8, :]


def start(copies):
    for copy in copies:
        copy.start()


def wait(copies):
    for copy in copies:
        copy.wait()


def copies_of(sources, targets, sems):
    return [
        pltpu.make_async_copy(source, target, sems.at[k])
        for k, (source, target) in enumerate(zip(sources, targets))
    ]


def put_slots(table, first, tmp, total):
    for slot in range(4):
        put_rows(table, first + 16 * slot, tmp[128 * slot : 128 * slot + 128, :], total)


def add_product(tmp, step, rows, columns):
    product = jnp.dot(rows, columns, preferred_element_type=jnp.float32)
    tmp[...] = tmp[...] + product if step else product


class Stages:
    def __init__(self, stages, sems):
        self.copies = []
        for number, (sources, targets) in enumerate(stages):
            self.copies.append(copies_of(sources, targets, sems.at[number]))
        for number in range(3):
            self.start(number)

    def start(self, number):
        if number < len(self.copies):
            start(self.copies[number])

    def wait(self, number):
        wait(self.copies[number])
        self.start(number + 3)


def own_kernel(table, *refs):
    pieces, (head, head_2, info, mine, other, stats, xbuf, hbuf, tmp, sems) = refs[:8], refs[8:]
    stages = []
    for step in range(2 * WIDE // DEEP):
        cut = pl.ds(DEEP * step, DEEP)
        part, within = DEEP * step // WIDE, pl.ds(DEEP * step % WIDE, DEEP)
        sources = [piece.at[:, within] for piece in pieces[part::2]]
        targets = [xbuf.at[pl.ds(128 * k, 128), cut] for k in range(4)]
        stages.append((sources + [head.at[cut, :]], targets + [hbuf.at[0, cut, :]]))
        stages.append(([head_2.at[cut, :]], [hbuf.at[1, cut, :]]))
    stages = Stages(stages, sems)
    for step in range(2 * WIDE // DEEP):
        cut = slice(DEEP * step, DEEP * step + DEEP)
        for side in (0, 1):
            stages.wait(2 * step + side)
            add_product(tmp.at[side], step, xbuf[:, cut], hbuf[side, cut, :])
    for side, total in enumerate((mine, other)):
        put_slots(table, 0, tmp.at[side], total)
    write_stats((mine, other), info, stats)


def ref_kernel(table, *refs):
    pieces, (head, head_2, info, stats, xbuf, hbuf, tmp, total, sems) = refs[:4], refs[4:]
    stages = []
    for step in range(WIDE // DEEP):
        cut = pl.ds(DEEP * step, DEEP)
        sources = [piece.at[:, cut] for piece in pieces]
        targets = [xbuf.at[pl.ds(128 * k, 128), cut] for k in range(4)]
        stages.append((sources + [head.at[cut, :]], targets + [hbuf.at[0, cut, :]]))
        stages.append(([head_2.at[cut, :]], [hbuf.at[1, cut, :]]))
    stages = Stages(stages, sems)
    for step in range(WIDE // DEEP):
        cut = slice(DEEP * step, DEEP * step + DEEP)
        for side in (0, 1):
            stages.wait(2 * step + side)
            add_product(tmp.at[side], step, xbuf[:, cut], hbuf[side, cut, :])
    for side in (0, 1):
        put_slots(table, 128, tmp.at[side], total.at[side])
    write_stats((total.at[0], total.at[1]), info, stats)


def grad_kernel(table, *refs):
    pieces, (mine, other, lse, lse_2, info, out) = refs[:16], refs[16:22]
    xbuf, obuf, plain, ordered, scaled, sems, out_sems = refs[22:]
    logits = [
        pltpu.make_async_copy(source, plain.at[pl.ds(HALF * k, HALF), :], sems.at[2, k])
        for k, source in enumerate((mine, other))
    ]
    start(logits)
    arrive = []
    for part in (0, 1):
        sources = pieces[part::2]
        arrive.append(
            [
                pltpu.make_async_copy(
                    source, xbuf.at[part, pl.ds(128 * k, 128), :], sems.at[part, k]
                )
                for k, source in enumerate(sources)
            ]
        )
    start(arrive[0])
    wait(logits)
    column = lax.broadcasted_iota(jnp.int32, (128, HALF), 1).astype(jnp.float32)
    for step in range(2 * HALF // 128):
        rows = slice(128 * step, 128 * step + 128)
        told = jnp.transpose(info[:, rows])
        joined = lse[step : step + 1, :] if step < 4 else lse_2[step - 4 : step - 3, :]
        joined = jnp.transpose(jnp.broadcast_to(joined, (8, 128)))[:, 0:1]
        hit = (column == told[:, 0:1]).astype(jnp.float32)
        plain[rows, :] = told[:, 2:3] * (jnp.exp(plain[rows, :] - joined) - hit)
    for group in range(128):
        source = pl.multiple_of(table[group] + HALF * (group // 64), 8)
        ordered[8 * group : 8 * group + 8, :] = plain[pl.ds(source, 8), :]
    scaled[...] = ordered[...].astype(jnp.bfloat16)
    steps = WIDE // BLOCK
    sent = []
    for part in (0, 1):
        wait(arrive[part])
        if part == 0:
            start(arrive[1])
        for step in range(steps):
            number = part * steps + step
            if number >= 2:
                sent[number - 2].wait()
            obuf[number % 2] = lax.dot_general(
                xbuf[part, :, BLOCK * step : BLOCK * step + BLOCK],
                scaled[...],
                (((0,), (0,)), ((), ())),
                preferred_element_type=jnp.float32,
            ).astype(jnp.bfloat16)
            sent.append(
                pltpu.make_async_copy(
                    obuf.at[number % 2],
                    out.at[pl.ds(BLOCK * number, BLOCK), :],
                    out_sems.at[number % 2],
                )
            )
            sent[number].start()
    wait(sent[-2:])


ANY = pl.BlockSpec(memory_space=pl.ANY)
INSIDE = pl.BlockSpec(memory_space=pltpu.VMEM)
TABLE = pl.BlockSpec(memory_space=pltpu.SMEM)
DMA = pltpu.SemaphoreType.DMA


def floats(*shape):
    return jax.ShapeDtypeStruct(shape, jnp.float32)


def call(kernel, operands, out_shape, out_specs, scratch, rows, specs):
    return pl.pallas_call(
        kernel,
        out_shape=out_shape,
        in_specs=[TABLE, *specs],
        out_specs=out_specs,
        scratch_shapes=scratch,
        compiler_params=pltpu.CompilerParams(vmem_limit_bytes=60 * MIB),
        cost_estimate=pl.CostEstimate(
            flops=4 * rows * HALF * WIDE, bytes_accessed=12 * MIB, transcendentals=0
        ),
    )(*operands)


TOTALS = (floats(HALF, HALF), floats(HALF, HALF))


def own_call(table, pieces, heads, info):
    operands = (table, *pieces, *heads, info)
    shapes = (*TOTALS, floats(8, HALF))
    scratch = [
        pltpu.VMEM((HALF, 2 * WIDE), jnp.bfloat16),
        pltpu.VMEM((2, 2 * WIDE, HALF), jnp.bfloat16),
        pltpu.VMEM((2, HALF, HALF), jnp.float32),
        DMA((4 * WIDE // DEEP, 5)),
    ]
    specs = [ANY] * 10 + [INSIDE]
    return call(own_kernel, operands, shapes, (INSIDE,) * 3, scratch, 1024, specs)


def ref_call(table, pieces, heads, info):
    operands = (table, *pieces, *heads, info)
    scratch = [
        pltpu.VMEM((HALF, WIDE), jnp.bfloat16),
        pltpu.VMEM((2, WIDE, HALF), jnp.bfloat16),
        pltpu.VMEM((2, HALF, HALF), jnp.float32),
        pltpu.VMEM((2, HALF, HALF), jnp.float32),
        DMA((2 * WIDE // DEEP, 5)),
    ]
    specs = [ANY] * 6 + [INSIDE]
    return call(ref_kernel, operands, floats(8, HALF), INSIDE, scratch, 512, specs)


def grad_call(table, pieces, logits, lses, info):
    scratch = [
        pltpu.VMEM((2, 2 * HALF, WIDE), jnp.bfloat16),
        pltpu.VMEM((2, BLOCK, HALF), jnp.bfloat16),
        pltpu.VMEM((2 * HALF, HALF), jnp.float32),
        pltpu.VMEM((2 * HALF, HALF), jnp.float32),
        pltpu.VMEM((2 * HALF, HALF), jnp.bfloat16),
        DMA((3, 8)),
        DMA((2,)),
    ]
    operands = (table, *pieces, *logits, *lses, info)
    specs = [ANY] * 18 + [INSIDE] * 3
    shape = jax.ShapeDtypeStruct((2 * WIDE, HALF), jnp.bfloat16)
    return call(grad_kernel, operands, shape, ANY, scratch, 1024, specs)


def log_sum(terms, axis):
    peak = jnp.max(terms, axis=axis)
    return peak + jnp.log(jnp.sum(jnp.exp(terms - jnp.expand_dims(peak, axis)), axis=axis))


def core_tokens(values, core):
    values = values.reshape(64, 2, 8)
    return jnp.where(core == 0, values[:, 0], values[:, 1]).reshape(HALF)


def shards(
    ref_rows, ref_gain, trainee_rows, trainee_gain, ref_head, trainee_head, targets, selected
):
    me = lax.axis_index(ALL)
    core = lax.axis_index("c")
    chip = me // 2

    table = row_table(me)
    weight = selected.astype(jnp.float32)

    def info_of(which):
        wanted = core_tokens(targets, which)
        row = lax.broadcasted_iota(jnp.int32, (8, HALF), 0)
        beside = (wanted - HALF * (me ^ 1)).astype(jnp.float32)
        here = (wanted - HALF * me).astype(jnp.float32)
        rest = jnp.where(row == 1, beside[None], core_tokens(weight, which)[None])
        return jnp.where(row == 0, here[None], rest)

    info, info_2 = info_of(core), info_of(1 - core)

    raw = trainee_rows.reshape(2, 2, 8, 2048).transpose(1, 0, 2, 3).reshape(1, 1, 2, 16, 2048)
    raw = jnp.broadcast_to(raw, (2, 2, 2, 16, 2048)).reshape(8, 16, 2048)
    raw, ref = fence(raw, normalize(ref_rows, ref_gain))
    raw = lax.all_to_all(raw, ("zl", "zh", "c"), 0, 0, tiled=True).reshape(2, 4, 16, 2048)
    own = normalize(raw.transpose(0, 2, 1, 3).reshape(32, 2 * WIDE), trainee_gain)
    ref = stack(ring(stack(ring(ref, "xy")), "yx"))
    head_2, ref_head_2 = swap(trainee_head), swap(ref_head)
    own, ref, head_2, ref_head_2 = fence(own, ref, head_2, ref_head_2)
    heads, ref_heads = (trainee_head, head_2), (ref_head, ref_head_2)

    ref_near, ref_back = send(ref, "zz", (1, -1)), send(ref, "zz", (-1, 1))
    own = ring(own, "xy")
    low, top = fence(stack(own, slice(0, WIDE)), stack(own, slice(WIDE, None)))

    low_near, top_back = send(low, "yx", (1, 1)), send(top, "yx", (-1, -1))
    low, top, low_near, top_back, ref_near, ref_back = fence(
        low, top, low_near, top_back, ref_near, ref_back
    )

    low_far, top_far = send(low_near, "yx", (1, 1)), send(top_back, "yx", (-1, -1))
    top_near, low_back = send(top, "yx", (1, 1)), send(low, "yx", (-1, -1))
    ref_far = send(ref_near, "zz", (1, -1))
    ref_stats = ref_call(table, (ref, ref_near, ref_back, ref_far), ref_heads, info)
    pieces = (low, top, low_near, top_near, low_back, top_back, low_far, top_far)
    *pieces, ref_stats = fence(*pieces, ref_stats)

    swapped = [swap(piece) for piece in pieces[:5]]
    mine, other, stats = own_call(table, pieces, heads, info)

    rest = jnp.concatenate(
        [ref_stats[0].reshape(64, 8), (stats[1] - ref_stats[1]).reshape(64, 8)], axis=1
    )
    rest = jnp.pad(rest, ((0, 0), (0, 112)))
    message = jnp.concatenate(
        [jnp.broadcast_to(stats[0].reshape(1, 4, 128), (64, 4, 128)), rest[:, None]], axis=1
    )
    message, other, *swapped = fence(message, other, *swapped)
    swapped += [swap(piece) for piece in pieces[5:]]
    arrived = lax.all_to_all(message, CHIPS, 0, 0, tiled=True)
    other_2 = swap(other)
    lse = log_sum(arrived[:, :4], 0)
    lse_2 = swap(lse)
    found = log_sum(arrived[:, 4, :8], 0)
    hits = jnp.sum(arrived[:, 4, 8:16], axis=0)
    excess = lax.dynamic_slice_in_dim(lse.reshape(HALF), 8 * chip, 8) - found - hits

    both = jnp.concatenate([info, info_2], axis=1)
    head_grad = grad_call(table, (*pieces, *swapped), (mine, other_2), (lse, lse_2), both)
    return excess, head_grad


def solution(mesh):
    grid = Mesh(mesh.devices.reshape(4, 2, 4, 2, 2), ALL)
    in_specs = (P(ALL, None), P(), P(FSDP, TP), P(), P(None, ALL), P(None, ALL), P(), P())
    out_specs = (P(ALL), P(None, ALL))
    return jax.shard_map(shards, mesh=grid, in_specs=in_specs, out_specs=out_specs, check_vma=False)
```

```python
import jax
import jax.numpy as jnp
from jax import lax
from jax.experimental import pallas as pl
from jax.experimental.pallas import tpu as pltpu
from jax.sharding import Mesh
from jax.sharding import PartitionSpec as P

EPSILON = 1e-05
FSDP = ("y", "zl", "x")
TP = ("zh", "c")
ALL = (*FSDP, *TP)
CHIPS = ALL[:-1]
WIDE = 4096
HALF = 512
BLOCK = 1024
DEEP = 2048
FIRST = 448
OWN_STEPS = ((0, 1024), (1024, 3072), (4096, 4096))
MIB = 1 << 20


def flat(x, y, z, core):
    return (((y % 4) * 2 + (z % 4) % 2) * 4 + (x % 4)) * 4 + ((z % 4) // 2) * 2 + core


def place(index):
    x = (index // 4) % 4
    y = index // 32
    z = ((index // 2) % 2) * 2 + (index // 16) % 2
    return x, y, z, index % 2


def send(values, axes, steps):
    pairs = []
    for index in range(128):
        x, y, z, core = place(index)
        at = {"x": x, "y": y, "z": z}
        at[axes[core]] += steps[core]
        pairs.append((index, flat(at["x"], at["y"], at["z"], core)))
    return lax.ppermute(values, ALL, pairs)


def swap(values):
    return lax.ppermute(values, ALL, [(index, index ^ 1) for index in range(128)])


def ring(rows, axes):
    return [rows, *(send(rows, axes, (steps, steps)) for steps in (1, -1, 2))]


def stack(pieces, cut=slice(None)):
    return jnp.concatenate([piece[:, cut] for piece in pieces], axis=0)


def fence(*values):
    return lax.optimization_barrier(values)


def normalize(values, gain):
    widened = values.astype(jnp.float32)
    factor = lax.rsqrt(jnp.mean(widened * widened, axis=1, keepdims=True) + EPSILON)
    return (widened * factor * gain).astype(jnp.bfloat16)


def row_table(me):
    x, y, z, mine = place(me)
    t = jnp.arange(2 * 8 * 16, dtype=jnp.int32)
    part, slot, group = t // 128, (t // 16) % 8, t % 16
    core = jnp.where(slot >= 4, 1 - mine, mine)

    def offset(j):
        return jnp.where(j == 0, 0, jnp.where(j == 3, 2, 2 * j - 3)) + 4

    last, outer, inner = offset(slot % 4), offset(group // 4), offset(group % 4)
    first, second = jnp.where(part == 0, outer, inner), jnp.where(part == 0, last, outer)
    at_x = (x + jnp.where(core == 0, first, second)) % 4
    at_y = (y + jnp.where(core == 0, second, first)) % 4
    at_z = (z + jnp.where(core == 0, last, 8 - last)) % 4
    low = jnp.where(part == 1, at_z % 2, group // 2 % 2)
    high = jnp.where(part == 1, at_z // 2, group % 2)
    return 8 * (((at_y * 2 + low) * 4 + at_x) * 2 + high)


def put_rows(table, first, values, total):
    for group in range(16):
        target = pl.ds(pl.multiple_of(table[first + group], 8), 8)
        total[target, :] = values[8 * group : 8 * group + 8, :]


def write_stats(sides, info, stats):
    column = lax.broadcasted_iota(jnp.int32, (128, HALF), 1).astype(jnp.float32)
    lane = lax.broadcasted_iota(jnp.int32, (128, 128), 1)
    for step in range(HALF // 128):
        rows = slice(128 * step, 128 * step + 128)
        told = jnp.transpose(info[:, rows])
        values = [side[rows, :] for side in sides]
        peaks = [jnp.max(value, axis=1, keepdims=True) for value in values]
        peak = jnp.maximum(*peaks)
        summed = jnp.sum(sum(jnp.exp(value - peak) for value in values), axis=1, keepdims=True)
        hits = [
            jnp.where(column == told[:, number : number + 1], value, 0.0)
            for number, value in enumerate(values)
        ]
        hit = jnp.sum(sum(hits), axis=1, keepdims=True)
        block = jnp.where(lane == 0, peak + jnp.log(summed), jnp.where(lane == 1, hit, 0.0))
        stats[:, rows] = jnp.transpose(block)[0:8, :]


def start(copies):
    for copy in copies:
        copy.start()


def wait(copies):
    for copy in copies:
        copy.wait()


def copies_of(sources, targets, sems):
    return [
        pltpu.make_async_copy(source, target, sems.at[k])
        for k, (source, target) in enumerate(zip(sources, targets))
    ]


def put_slots(table, first, tmp, total):
    for slot in range(4):
        put_rows(table, first + 16 * slot, tmp[128 * slot : 128 * slot + 128, :], total)


def add_product(tmp, step, rows, columns):
    product = jnp.dot(rows, columns, preferred_element_type=jnp.float32)
    tmp[...] = tmp[...] + product if step else product


class Stages:
    def __init__(self, stages, sems):
        self.copies = []
        for number, (sources, targets) in enumerate(stages):
            self.copies.append(copies_of(sources, targets, sems.at[number]))
        for number in range(3):
            self.start(number)

    def start(self, number):
        if number < len(self.copies):
            start(self.copies[number])

    def wait(self, number):
        wait(self.copies[number])
        self.start(number + 3)


def own_kernel(table, *refs):
    pieces, (head, head_2, info, mine, other, stats, xbuf, hbuf, tmp, sems) = refs[:8], refs[8:]
    stages = []
    for first, depth in OWN_STEPS:
        cut, part, within = pl.ds(first, depth), first // WIDE, pl.ds(first % WIDE, depth)
        sources = [piece.at[:, within] for piece in pieces[part::2]]
        targets = [xbuf.at[pl.ds(128 * k, 128), cut] for k in range(4)]
        stages.append((sources + [head.at[cut, :]], targets + [hbuf.at[0, cut, :]]))
        stages.append(([head_2.at[cut, :]], [hbuf.at[1, cut, :]]))
    stages = Stages(stages, sems)
    for step, (first, depth) in enumerate(OWN_STEPS):
        cut = slice(first, first + depth)
        for side in (0, 1):
            stages.wait(2 * step + side)
            add_product(tmp.at[side], step, xbuf[:, cut], hbuf[side, cut, :])
    for side, total in enumerate((mine, other)):
        put_slots(table, 0, tmp.at[side], total)
    write_stats((mine, other), info, stats)


def ref_kernel(table, *refs):
    pieces, (head, first_2, head_2, info, stats, xbuf, hbuf, tmp, total, sems) = refs[:4], refs[4:]
    stages = []
    for step in range(WIDE // DEEP):
        cut = pl.ds(DEEP * step, DEEP)
        sources = [piece.at[:, cut] for piece in pieces]
        targets = [xbuf.at[pl.ds(128 * k, 128), cut] for k in range(4)]
        stages.append((sources + [head.at[cut, :]], targets + [hbuf.at[0, cut, :]]))
        sources, targets = [head_2.at[cut, :]], [hbuf.at[1, cut, :]]
        if step == 0:
            rest = pl.ds(FIRST, DEEP - FIRST)
            sources = [first_2, head_2.at[rest, :]]
            targets = [hbuf.at[1, pl.ds(0, FIRST), :], hbuf.at[1, rest, :]]
        stages.append((sources, targets))
    stages = Stages(stages, sems)
    for step in range(WIDE // DEEP):
        cut = slice(DEEP * step, DEEP * step + DEEP)
        for side in (0, 1):
            stages.wait(2 * step + side)
            add_product(tmp.at[side], step, xbuf[:, cut], hbuf[side, cut, :])
    for side in (0, 1):
        put_slots(table, 128, tmp.at[side], total.at[side])
    write_stats((total.at[0], total.at[1]), info, stats)


def grad_kernel(table, *refs):
    pieces, (mine, other, lse, lse_2, info, out) = refs[:16], refs[16:22]
    xbuf, obuf, plain, ordered, scaled, sems, out_sems = refs[22:]
    logits = [
        pltpu.make_async_copy(source, plain.at[pl.ds(HALF * k, HALF), :], sems.at[2, k])
        for k, source in enumerate((mine, other))
    ]
    start(logits)
    arrive = []
    for part in (0, 1):
        sources = pieces[part::2]
        arrive.append(
            [
                pltpu.make_async_copy(
                    source, xbuf.at[part, pl.ds(128 * k, 128), :], sems.at[part, k]
                )
                for k, source in enumerate(sources)
            ]
        )
    start(arrive[0])
    wait(logits)
    column = lax.broadcasted_iota(jnp.int32, (128, HALF), 1).astype(jnp.float32)
    for step in range(2 * HALF // 128):
        rows = slice(128 * step, 128 * step + 128)
        told = jnp.transpose(info[:, rows])
        joined = lse[step : step + 1, :] if step < 4 else lse_2[step - 4 : step - 3, :]
        joined = jnp.transpose(jnp.broadcast_to(joined, (8, 128)))[:, 0:1]
        hit = (column == told[:, 0:1]).astype(jnp.float32)
        plain[rows, :] = told[:, 2:3] * (jnp.exp(plain[rows, :] - joined) - hit)
    for group in range(128):
        source = pl.multiple_of(table[group] + HALF * (group // 64), 8)
        ordered[8 * group : 8 * group + 8, :] = plain[pl.ds(source, 8), :]
    scaled[...] = ordered[...].astype(jnp.bfloat16)
    steps = WIDE // BLOCK
    sent = []
    for part in (0, 1):
        wait(arrive[part])
        if part == 0:
            start(arrive[1])
        for step in range(steps):
            number = part * steps + step
            if number >= 2:
                sent[number - 2].wait()
            obuf[number % 2] = lax.dot_general(
                xbuf[part, :, BLOCK * step : BLOCK * step + BLOCK],
                scaled[...],
                (((0,), (0,)), ((), ())),
                preferred_element_type=jnp.float32,
            ).astype(jnp.bfloat16)
            sent.append(
                pltpu.make_async_copy(
                    obuf.at[number % 2],
                    out.at[pl.ds(BLOCK * number, BLOCK), :],
                    out_sems.at[number % 2],
                )
            )
            sent[number].start()
    wait(sent[-2:])


ANY = pl.BlockSpec(memory_space=pl.ANY)
INSIDE = pl.BlockSpec(memory_space=pltpu.VMEM)
TABLE = pl.BlockSpec(memory_space=pltpu.SMEM)
DMA = pltpu.SemaphoreType.DMA


def floats(*shape):
    return jax.ShapeDtypeStruct(shape, jnp.float32)


def call(kernel, operands, out_shape, out_specs, scratch, rows, specs, limit=60):
    return pl.pallas_call(
        kernel,
        out_shape=out_shape,
        in_specs=[TABLE, *specs],
        out_specs=out_specs,
        scratch_shapes=scratch,
        compiler_params=pltpu.CompilerParams(vmem_limit_bytes=limit * MIB),
        cost_estimate=pl.CostEstimate(
            flops=4 * rows * HALF * WIDE, bytes_accessed=12 * MIB, transcendentals=0
        ),
    )(*operands)


TOTALS = (floats(HALF, HALF), floats(HALF, HALF))


def own_call(table, pieces, heads, info):
    operands = (table, *pieces, *heads, info)
    shapes = (*TOTALS, floats(8, HALF))
    scratch = [
        pltpu.VMEM((HALF, 2 * WIDE), jnp.bfloat16),
        pltpu.VMEM((2, 2 * WIDE, HALF), jnp.bfloat16),
        pltpu.VMEM((2, HALF, HALF), jnp.float32),
        DMA((2 * len(OWN_STEPS), 5)),
    ]
    specs = [ANY] * 10 + [INSIDE]
    return call(own_kernel, operands, shapes, (INSIDE,) * 3, scratch, 1024, specs)


def ref_call(table, pieces, heads, info):
    operands = (table, *pieces, *heads, info)
    scratch = [
        pltpu.VMEM((HALF, WIDE), jnp.bfloat16),
        pltpu.VMEM((2, WIDE, HALF), jnp.bfloat16),
        pltpu.VMEM((2, HALF, HALF), jnp.float32),
        pltpu.VMEM((2, HALF, HALF), jnp.float32),
        DMA((2 * WIDE // DEEP, 5)),
    ]
    specs = [ANY] * 7 + [INSIDE]
    return call(ref_kernel, operands, floats(8, HALF), INSIDE, scratch, 512, specs)


def grad_call(table, pieces, logits, lses, info):
    scratch = [
        pltpu.VMEM((2, 2 * HALF, WIDE), jnp.bfloat16),
        pltpu.VMEM((2, BLOCK, HALF), jnp.bfloat16),
        pltpu.VMEM((2 * HALF, HALF), jnp.float32),
        pltpu.VMEM((2 * HALF, HALF), jnp.float32),
        pltpu.VMEM((2 * HALF, HALF), jnp.bfloat16),
        DMA((3, 8)),
        DMA((2,)),
    ]
    operands = (table, *pieces, *logits, *lses, info)
    specs = [ANY] * 18 + [INSIDE] * 3
    shape = jax.ShapeDtypeStruct((2 * WIDE, HALF), jnp.bfloat16)
    return call(grad_kernel, operands, shape, ANY, scratch, 1024, specs, 58)


def log_sum(terms, axis):
    peak = jnp.max(terms, axis=axis)
    return peak + jnp.log(jnp.sum(jnp.exp(terms - jnp.expand_dims(peak, axis)), axis=axis))


def core_tokens(values, core):
    values = values.reshape(64, 2, 8)
    return jnp.where(core == 0, values[:, 0], values[:, 1]).reshape(HALF)


def shards(
    ref_rows, ref_gain, trainee_rows, trainee_gain, ref_head, trainee_head, targets, selected
):
    me = lax.axis_index(ALL)
    core = lax.axis_index("c")
    chip = me // 2

    table = row_table(me)
    weight = selected.astype(jnp.float32)

    def info_of(which):
        wanted = core_tokens(targets, which)
        row = lax.broadcasted_iota(jnp.int32, (8, HALF), 0)
        beside = (wanted - HALF * (me ^ 1)).astype(jnp.float32)
        here = (wanted - HALF * me).astype(jnp.float32)
        rest = jnp.where(row == 1, beside[None], core_tokens(weight, which)[None])
        return jnp.where(row == 0, here[None], rest)

    info, info_2 = info_of(core), info_of(1 - core)

    raw = trainee_rows.reshape(2, 2, 8, 2048).transpose(1, 0, 2, 3).reshape(1, 1, 2, 16, 2048)
    raw = jnp.broadcast_to(raw, (2, 2, 2, 16, 2048)).reshape(8, 16, 2048)
    raw, ref = fence(raw, normalize(ref_rows, ref_gain))
    raw = lax.all_to_all(raw, ("zl", "zh", "c"), 0, 0, tiled=True).reshape(2, 4, 16, 2048)
    own = normalize(raw.transpose(0, 2, 1, 3).reshape(32, 2 * WIDE), trainee_gain)
    ref, first_2 = fence(stack(ring(ref, "xy")), swap(ref_head[:FIRST]))
    ref = stack(ring(ref, "yx"))
    head_2, ref_head_2 = swap(trainee_head), swap(ref_head)
    own, ref, head_2, ref_head_2 = fence(own, ref, head_2, ref_head_2)
    heads, ref_heads = (trainee_head, head_2), (ref_head, first_2, ref_head_2)

    ref_near, ref_back = send(ref, "zz", (1, -1)), send(ref, "zz", (-1, 1))
    own = ring(own, "xy")
    low, top = fence(stack(own, slice(0, WIDE)), stack(own, slice(WIDE, None)))

    low_near, top_back = send(low, "yx", (1, 1)), send(top, "yx", (-1, -1))
    low, top, low_near, top_back, ref_near, ref_back = fence(
        low, top, low_near, top_back, ref_near, ref_back
    )

    low_far, top_far = send(low_near, "yx", (1, 1)), send(top_back, "yx", (-1, -1))
    top_near, low_back = send(top, "yx", (1, 1)), send(low, "yx", (-1, -1))
    ref_far = send(ref_near, "zz", (1, -1))
    ref_stats = ref_call(table, (ref, ref_near, ref_back, ref_far), ref_heads, info)
    pieces = (low, top, low_near, top_near, low_back, top_back, low_far, top_far)
    *pieces, ref_stats = fence(*pieces, ref_stats)

    swapped = [swap(piece) for piece in pieces[:5]]
    mine, other, stats = own_call(table, pieces, heads, info)

    rest = jnp.stack([ref_stats[0], stats[1] - ref_stats[1]]).reshape(2, 4, 1, 128)
    rest = jnp.broadcast_to(rest, (2, 4, 16, 128)).reshape(2, 64, 1, 128)
    whole = jnp.broadcast_to(stats[0].reshape(1, 4, 128), (64, 4, 128))
    message = jnp.concatenate([whole, rest[0], rest[1]], axis=1)
    message, other, *swapped = fence(message, other, *swapped)
    swapped += [swap(piece) for piece in pieces[5:]]
    arrived = lax.all_to_all(message, CHIPS, 0, 0, tiled=True)
    other_2 = swap(other)
    lse = log_sum(arrived[:, :4], 0)
    lse_2 = swap(lse)
    rest = log_sum(arrived[:, 4], 0) + jnp.sum(arrived[:, 5], axis=0)
    rest = lax.dynamic_slice_in_dim(rest, 8 * (chip % 16), 8)
    excess = lax.dynamic_slice_in_dim(lse.reshape(HALF), 8 * chip, 8) - rest

    both = jnp.concatenate([info, info_2], axis=1)
    head_grad = grad_call(table, (*pieces, *swapped), (mine, other_2), (lse, lse_2), both)
    return excess, head_grad


def solution(mesh):
    grid = Mesh(mesh.devices.reshape(4, 2, 4, 2, 2), ALL)
    in_specs = (P(ALL, None), P(), P(FSDP, TP), P(), P(None, ALL), P(None, ALL), P(), P())
    out_specs = (P(ALL), P(None, ALL))
    return jax.shard_map(shards, mesh=grid, in_specs=in_specs, out_specs=out_specs, check_vma=False)
```

```python
import jax
import jax.numpy as jnp
from jax import lax
from jax.experimental import pallas as pl
from jax.experimental.pallas import tpu as pltpu
from jax.sharding import Mesh
from jax.sharding import PartitionSpec as P

EPSILON = 1e-05
FSDP = ("y", "zl", "x")
TP = ("zh", "c")
ALL = (*FSDP, *TP)
CHIPS = ALL[:-1]
WIDE = 4096
HALF = 512
BLOCK = 1024
DEEP = 2048
FIRST = 448
MIB = 1 << 20


def flat(x, y, z, core):
    return (((y % 4) * 2 + (z % 4) % 2) * 4 + (x % 4)) * 4 + ((z % 4) // 2) * 2 + core


def place(index):
    x = (index // 4) % 4
    y = index // 32
    z = ((index // 2) % 2) * 2 + (index // 16) % 2
    return x, y, z, index % 2


def send(values, axes, steps):
    pairs = []
    for index in range(128):
        x, y, z, core = place(index)
        at = {"x": x, "y": y, "z": z}
        at[axes[core]] += steps[core]
        pairs.append((index, flat(at["x"], at["y"], at["z"], core)))
    return lax.ppermute(values, ALL, pairs)


def swap(values):
    return lax.ppermute(values, ALL, [(index, index ^ 1) for index in range(128)])


def ring(rows, axes):
    return [rows, *(send(rows, axes, (steps, steps)) for steps in (1, -1, 2))]


def stack(pieces, cut=slice(None)):
    return jnp.concatenate([piece[:, cut] for piece in pieces], axis=0)


def fence(*values):
    return lax.optimization_barrier(values)


def normalize(values, gain):
    widened = values.astype(jnp.float32)
    factor = lax.rsqrt(jnp.mean(widened * widened, axis=1, keepdims=True) + EPSILON)
    return (widened * factor * gain).astype(jnp.bfloat16)


def row_table(me):
    x, y, z, mine = place(me)
    t = jnp.arange(2 * 8 * 16, dtype=jnp.int32)
    part, slot, group = t // 128, (t // 16) % 8, t % 16
    core = jnp.where(slot >= 4, 1 - mine, mine)

    def offset(j):
        return jnp.where(j == 0, 0, jnp.where(j == 3, 2, 2 * j - 3)) + 4

    last, outer, inner = offset(slot % 4), offset(group // 4), offset(group % 4)
    first, second = jnp.where(part == 0, outer, inner), jnp.where(part == 0, last, outer)
    at_x = (x + jnp.where(core == 0, first, second)) % 4
    at_y = (y + jnp.where(core == 0, second, first)) % 4
    at_z = (z + jnp.where(core == 0, last, 8 - last)) % 4
    low = jnp.where(part == 1, at_z % 2, group // 2 % 2)
    high = jnp.where(part == 1, at_z // 2, group % 2)
    return 8 * (((at_y * 2 + low) * 4 + at_x) * 2 + high)


def put_rows(table, first, values, total):
    for group in range(16):
        target = pl.ds(pl.multiple_of(table[first + group], 8), 8)
        total[target, :] = values[8 * group : 8 * group + 8, :]


def write_stats(sides, info, stats):
    column = lax.broadcasted_iota(jnp.int32, (128, HALF), 1).astype(jnp.float32)
    lane = lax.broadcasted_iota(jnp.int32, (128, 128), 1)
    for step in range(HALF // 128):
        rows = slice(128 * step, 128 * step + 128)
        told = jnp.transpose(info[:, rows])
        values = [side[rows, :] for side in sides]
        peaks = [jnp.max(value, axis=1, keepdims=True) for value in values]
        peak = jnp.maximum(*peaks)
        summed = jnp.sum(sum(jnp.exp(value - peak) for value in values), axis=1, keepdims=True)
        hits = [
            jnp.where(column == told[:, number : number + 1], value, 0.0)
            for number, value in enumerate(values)
        ]
        hit = jnp.sum(sum(hits), axis=1, keepdims=True)
        block = jnp.where(lane == 0, peak + jnp.log(summed), jnp.where(lane == 1, hit, 0.0))
        stats[:, rows] = jnp.transpose(block)[0:8, :]


def start(copies):
    for copy in copies:
        copy.start()


def wait(copies):
    for copy in copies:
        copy.wait()


def copies_of(sources, targets, sems):
    return [
        pltpu.make_async_copy(source, target, sems.at[k])
        for k, (source, target) in enumerate(zip(sources, targets))
    ]


def put_slots(table, first, tmp, total):
    for slot in range(4):
        put_rows(table, first + 16 * slot, tmp[128 * slot : 128 * slot + 128, :], total)


def add_product(tmp, step, rows, columns):
    product = jnp.dot(rows, columns, preferred_element_type=jnp.float32)
    tmp[...] = tmp[...] + product if step else product


class Stages:
    def __init__(self, stages, sems):
        self.copies = []
        for number, (sources, targets) in enumerate(stages):
            self.copies.append(copies_of(sources, targets, sems.at[number]))
        for number in range(3):
            self.start(number)

    def start(self, number):
        if number < len(self.copies):
            start(self.copies[number])

    def wait(self, number):
        wait(self.copies[number])
        self.start(number + 3)


def half_products(low, top, heads, xbuf, hbuf, tmp, sems):
    stages = []
    for step in range(2 * WIDE // DEEP):
        cut = pl.ds(DEEP * step, DEEP)
        part, within = DEEP * step // WIDE, pl.ds(DEEP * step % WIDE, DEEP)
        sources = [piece.at[:, within] for piece in (low, top)[part]]
        targets = [xbuf.at[pl.ds(128 * k, 128), cut] for k in (0, 1)]
        stages.append((sources + [heads[0].at[cut, :]], targets + [hbuf.at[0, cut, :]]))
        stages.append(([heads[1].at[cut, :]], [hbuf.at[1, cut, :]]))
    stages = Stages(stages, sems)
    for step in range(2 * WIDE // DEEP):
        cut, part = slice(DEEP * step, DEEP * step + DEEP), DEEP * step // WIDE
        for side in (0, 1):
            stages.wait(2 * step + side)
            add_product(
                tmp.at[side, part], DEEP * step % WIDE, xbuf[:, cut], hbuf[side, cut, :]
            )


def early_kernel(low, low_near, top, top_back, head, head_2, out, xbuf, hbuf, sems):
    half_products((low, low_near), (top, top_back), (head, head_2), xbuf, hbuf, out, sems)


def late_kernel(table, *refs):
    low_back, low_far, top_near, top_far, head, head_2, before, info = refs[:8]
    mine, other, stats, xbuf, hbuf, tmp, first, sems, before_sem = refs[8:]
    copy = pltpu.make_async_copy(before, first, before_sem)
    copy.start()
    low, top = (low_back, low_far), (top_near, top_far)
    half_products(low, top, (head, head_2), xbuf, hbuf, tmp, sems)
    copy.wait()
    for side, total in enumerate((mine, other)):
        a, b = slice(0, 128), slice(128, 256)
        slots = (
            first[side, 0, a, :] + first[side, 1, a, :],
            first[side, 0, b, :] + tmp[side, 1, a, :],
            first[side, 1, b, :] + tmp[side, 0, a, :],
            tmp[side, 0, b, :] + tmp[side, 1, b, :],
        )
        for number, values in enumerate(slots):
            put_rows(table, 16 * number, values, total)
    write_stats((mine, other), info, stats)


def ref_kernel(table, *refs):
    pieces, (head, first_2, head_2, info, stats, xbuf, hbuf, tmp, total, sems) = refs[:4], refs[4:]
    stages = []
    for step in range(WIDE // DEEP):
        cut = pl.ds(DEEP * step, DEEP)
        sources = [piece.at[:, cut] for piece in pieces]
        targets = [xbuf.at[pl.ds(128 * k, 128), cut] for k in range(4)]
        stages.append((sources + [head.at[cut, :]], targets + [hbuf.at[0, cut, :]]))
        sources, targets = [head_2.at[cut, :]], [hbuf.at[1, cut, :]]
        if step == 0:
            rest = pl.ds(FIRST, DEEP - FIRST)
            sources = [first_2, head_2.at[rest, :]]
            targets = [hbuf.at[1, pl.ds(0, FIRST), :], hbuf.at[1, rest, :]]
        stages.append((sources, targets))
    stages = Stages(stages, sems)
    for step in range(WIDE // DEEP):
        cut = slice(DEEP * step, DEEP * step + DEEP)
        for side in (0, 1):
            stages.wait(2 * step + side)
            add_product(tmp.at[side], step, xbuf[:, cut], hbuf[side, cut, :])
    for side in (0, 1):
        put_slots(table, 128, tmp.at[side], total.at[side])
    write_stats((total.at[0], total.at[1]), info, stats)


def grad_kernel(table, *refs):
    pieces, (mine, other, lse, lse_2, info, out) = refs[:16], refs[16:22]
    xbuf, obuf, plain, ordered, scaled, sems, out_sems = refs[22:]
    logits = [
        pltpu.make_async_copy(source, plain.at[pl.ds(HALF * k, HALF), :], sems.at[2, k])
        for k, source in enumerate((mine, other))
    ]
    start(logits)
    arrive = []
    for part in (0, 1):
        sources = pieces[part::2]
        arrive.append(
            [
                pltpu.make_async_copy(
                    source, xbuf.at[part, pl.ds(128 * k, 128), :], sems.at[part, k]
                )
                for k, source in enumerate(sources)
            ]
        )
    start(arrive[0])
    wait(logits)
    column = lax.broadcasted_iota(jnp.int32, (128, HALF), 1).astype(jnp.float32)
    for step in range(2 * HALF // 128):
        rows = slice(128 * step, 128 * step + 128)
        told = jnp.transpose(info[:, rows])
        joined = lse[step : step + 1, :] if step < 4 else lse_2[step - 4 : step - 3, :]
        joined = jnp.transpose(jnp.broadcast_to(joined, (8, 128)))[:, 0:1]
        hit = (column == told[:, 0:1]).astype(jnp.float32)
        plain[rows, :] = told[:, 2:3] * (jnp.exp(plain[rows, :] - joined) - hit)
    for group in range(128):
        source = pl.multiple_of(table[group] + HALF * (group // 64), 8)
        ordered[8 * group : 8 * group + 8, :] = plain[pl.ds(source, 8), :]
    scaled[...] = ordered[...].astype(jnp.bfloat16)
    steps = WIDE // BLOCK
    sent = []
    for part in (0, 1):
        wait(arrive[part])
        if part == 0:
            start(arrive[1])
        for step in range(steps):
            number = part * steps + step
            if number >= 2:
                sent[number - 2].wait()
            obuf[number % 2] = lax.dot_general(
                xbuf[part, :, BLOCK * step : BLOCK * step + BLOCK],
                scaled[...],
                (((0,), (0,)), ((), ())),
                preferred_element_type=jnp.float32,
            ).astype(jnp.bfloat16)
            sent.append(
                pltpu.make_async_copy(
                    obuf.at[number % 2],
                    out.at[pl.ds(BLOCK * number, BLOCK), :],
                    out_sems.at[number % 2],
                )
            )
            sent[number].start()
    wait(sent[-2:])


ANY = pl.BlockSpec(memory_space=pl.ANY)
INSIDE = pl.BlockSpec(memory_space=pltpu.VMEM)
TABLE = pl.BlockSpec(memory_space=pltpu.SMEM)
DMA = pltpu.SemaphoreType.DMA


def floats(*shape):
    return jax.ShapeDtypeStruct(shape, jnp.float32)


def call(kernel, operands, out_shape, out_specs, scratch, rows, specs):
    return pl.pallas_call(
        kernel,
        out_shape=out_shape,
        in_specs=specs,
        out_specs=out_specs,
        scratch_shapes=scratch,
        compiler_params=pltpu.CompilerParams(vmem_limit_bytes=60 * MIB),
        cost_estimate=pl.CostEstimate(
            flops=4 * rows * HALF * WIDE, bytes_accessed=12 * MIB, transcendentals=0
        ),
    )(*operands)


TOTALS = (floats(HALF, HALF), floats(HALF, HALF))


PARTIAL = (2, 2, 256, HALF)


def half_scratch():
    return [
        pltpu.VMEM((256, 2 * WIDE), jnp.bfloat16),
        pltpu.VMEM((2, 2 * WIDE, HALF), jnp.bfloat16),
    ]


def early_call(pieces, heads):
    scratch = [*half_scratch(), DMA((4 * WIDE // DEEP, 3))]
    return call(early_kernel, (*pieces, *heads), floats(*PARTIAL), INSIDE, scratch, 512, [ANY] * 6)


def late_call(table, pieces, heads, before, info):
    operands = (table, *pieces, *heads, before, info)
    shapes = (*TOTALS, floats(8, HALF))
    scratch = [
        *half_scratch(),
        pltpu.VMEM(PARTIAL, jnp.float32),
        pltpu.VMEM(PARTIAL, jnp.float32),
        DMA((4 * WIDE // DEEP, 3)),
        DMA,
    ]
    specs = [TABLE] + [ANY] * 7 + [INSIDE]
    return call(late_kernel, operands, shapes, (INSIDE,) * 3, scratch, 512, specs)


def ref_call(table, pieces, heads, info):
    operands = (table, *pieces, *heads, info)
    scratch = [
        pltpu.VMEM((HALF, WIDE), jnp.bfloat16),
        pltpu.VMEM((2, WIDE, HALF), jnp.bfloat16),
        pltpu.VMEM((2, HALF, HALF), jnp.float32),
        pltpu.VMEM((2, HALF, HALF), jnp.float32),
        DMA((2 * WIDE // DEEP, 5)),
    ]
    specs = [TABLE] + [ANY] * 7 + [INSIDE]
    return call(ref_kernel, operands, floats(8, HALF), INSIDE, scratch, 512, specs)


def grad_call(table, pieces, logits, lses, info):
    scratch = [
        pltpu.VMEM((2, 2 * HALF, WIDE), jnp.bfloat16),
        pltpu.VMEM((2, BLOCK, HALF), jnp.bfloat16),
        pltpu.VMEM((2 * HALF, HALF), jnp.float32),
        pltpu.VMEM((2 * HALF, HALF), jnp.float32),
        pltpu.VMEM((2 * HALF, HALF), jnp.bfloat16),
        DMA((3, 8)),
        DMA((2,)),
    ]
    operands = (table, *pieces, *logits, *lses, info)
    specs = [TABLE] + [ANY] * 18 + [INSIDE] * 3
    shape = jax.ShapeDtypeStruct((2 * WIDE, HALF), jnp.bfloat16)
    return call(grad_kernel, operands, shape, ANY, scratch, 1024, specs)


def log_sum(terms, axis):
    peak = jnp.max(terms, axis=axis)
    return peak + jnp.log(jnp.sum(jnp.exp(terms - jnp.expand_dims(peak, axis)), axis=axis))


def core_tokens(values, core):
    values = values.reshape(64, 2, 8)
    return jnp.where(core == 0, values[:, 0], values[:, 1]).reshape(HALF)


def shards(
    ref_rows, ref_gain, trainee_rows, trainee_gain, ref_head, trainee_head, targets, selected
):
    me = lax.axis_index(ALL)
    core = lax.axis_index("c")
    chip = me // 2

    table = row_table(me)
    weight = selected.astype(jnp.float32)

    def info_of(which):
        wanted = core_tokens(targets, which)
        row = lax.broadcasted_iota(jnp.int32, (8, HALF), 0)
        beside = (wanted - HALF * (me ^ 1)).astype(jnp.float32)
        here = (wanted - HALF * me).astype(jnp.float32)
        rest = jnp.where(row == 1, beside[None], core_tokens(weight, which)[None])
        return jnp.where(row == 0, here[None], rest)

    info, info_2 = info_of(core), info_of(1 - core)

    raw = trainee_rows.reshape(2, 2, 8, 2048).transpose(1, 0, 2, 3).reshape(1, 1, 2, 16, 2048)
    raw = jnp.broadcast_to(raw, (2, 2, 2, 16, 2048)).reshape(8, 16, 2048)
    raw, ref = fence(raw, normalize(ref_rows, ref_gain))
    raw = lax.all_to_all(raw, ("zl", "zh", "c"), 0, 0, tiled=True).reshape(2, 4, 16, 2048)
    own = normalize(raw.transpose(0, 2, 1, 3).reshape(32, 2 * WIDE), trainee_gain)
    ref, first_2 = fence(stack(ring(ref, "xy")), swap(ref_head[:FIRST]))
    ref = stack(ring(ref, "yx"))
    head_2, ref_head_2 = swap(trainee_head), swap(ref_head)
    own, ref, head_2, ref_head_2 = fence(own, ref, head_2, ref_head_2)
    heads, ref_heads = (trainee_head, head_2), (ref_head, first_2, ref_head_2)

    ref_near, ref_back = send(ref, "zz", (1, -1)), send(ref, "zz", (-1, 1))
    own = ring(own, "xy")
    low, top = fence(stack(own, slice(0, WIDE)), stack(own, slice(WIDE, None)))

    low_near, top_back = send(low, "yx", (1, 1)), send(top, "yx", (-1, -1))
    low, top, low_near, top_back, ref_near, ref_back = fence(
        low, top, low_near, top_back, ref_near, ref_back
    )

    low_far, top_far = send(low_near, "yx", (1, 1)), send(top_back, "yx", (-1, -1))
    top_near, low_back = send(top, "yx", (1, 1)), send(low, "yx", (-1, -1))
    ref_far = send(ref_near, "zz", (1, -1))
    ref_stats = ref_call(table, (ref, ref_near, ref_back, ref_far), ref_heads, info)
    before = early_call((low, low_near, top, top_back), heads)
    pieces = (low, top, low_near, top_near, low_back, top_back, low_far, top_far)
    *pieces, ref_stats, before = fence(*pieces, ref_stats, before)

    swapped = [swap(piece) for piece in pieces[:5]]
    late = (pieces[4], pieces[6], pieces[3], pieces[7])
    mine, other, stats = late_call(table, late, heads, before, info)

    rest = jnp.stack([ref_stats[0], stats[1] - ref_stats[1]]).reshape(2, 4, 1, 128)
    rest = jnp.broadcast_to(rest, (2, 4, 16, 128)).reshape(2, 64, 128)
    message = jnp.concatenate(
        [jnp.broadcast_to(stats[0].reshape(1, 4, 128), (64, 4, 128)), rest[0][:, None], rest[1][:, None]],
        axis=1,
    )
    message, other, *swapped = fence(message, other, *swapped)
    swapped += [swap(piece) for piece in pieces[5:]]
    arrived = lax.all_to_all(message, CHIPS, 0, 0, tiled=True)
    other_2 = swap(other)
    lse = log_sum(arrived[:, :4], 0)
    lse_2 = swap(lse)
    rest = log_sum(arrived[:, 4], 0) + jnp.sum(arrived[:, 5], axis=0)
    rest = lax.dynamic_slice_in_dim(rest, 8 * (chip % 16), 8)
    excess = lax.dynamic_slice_in_dim(lse.reshape(HALF), 8 * chip, 8) - rest

    both = jnp.concatenate([info, info_2], axis=1)
    head_grad = grad_call(table, (*pieces, *swapped), (mine, other_2), (lse, lse_2), both)
    return excess, head_grad


def solution(mesh):
    grid = Mesh(mesh.devices.reshape(4, 2, 4, 2, 2), ALL)
    in_specs = (P(ALL, None), P(), P(FSDP, TP), P(), P(None, ALL), P(None, ALL), P(), P())
    out_specs = (P(ALL), P(None, ALL))
    return jax.shard_map(shards, mesh=grid, in_specs=in_specs, out_specs=out_specs, check_vma=False)
```
